256 devices in a mesh: rep: 32 (over x, z), tp: 8 (over y, core).
Axes of the slice: x: 4, y: 4, z: 8, core: 2. Of those that a mesh axis runs over, the one named last changes fastest.
Arguments:
- res_state: bfloat16 [128, 128, 64, 128], P('rep', 'tp'), may hold values from -0.59765625 to 0.59765625
- res_conv_x: bfloat16 [128, 3, 8192], P('rep', None, 'tp'), may hold values from -6 to 6
- res_conv_bc: bfloat16 [128, 3, 2, 1024], P('rep', None, None, 'tp'), may hold values from -6 to 6
- res_x: bfloat16 [128, 64, 8192], P('rep', None, 'tp'), may hold values from -6 to 6
- res_bc: bfloat16 [128, 64, 2, 1024], P('rep', None, None, 'tp'), may hold values from -6 to 6
- res_z: bfloat16 [128, 64, 8192], P('rep', None, 'tp'), may hold values from -6 to 6
- res_dt: bfloat16 [128, 64, 128], P('rep', None, 'tp'), may hold values from -3 to 3
- res_count: int32 [32], P('rep'), may hold values from 1 to 4, as said below
- hand_state: bfloat16 [32, 128, 64, 128], P('rep', 'tp'), may hold values from -0.59765625 to 0.59765625
- hand_conv_x: bfloat16 [32, 3, 8192], P('rep', None, 'tp'), may hold values from -6 to 6
- hand_conv_bc: bfloat16 [32, 3, 2, 1024], P('rep', None, None, 'tp'), may hold values from -6 to 6
- slot_x: bfloat16 [96, 64, 8192], P('rep', None, 'tp'), may hold values from -6 to 6
- slot_bc: bfloat16 [96, 64, 2, 1024], P('rep', None, None, 'tp'), may hold values from -6 to 6
- slot_z: bfloat16 [96, 64, 8192], P('rep', None, 'tp'), may hold values from -6 to 6
- slot_dt: bfloat16 [96, 64, 128], P('rep', None, 'tp'), may hold values from -3 to 3
- assignment: int32 [32], replicated, may hold values from 0 to 31, as said below
- conv_wx: float32 [4, 8192], P(None, 'tp'), may hold values from -3 to 3
- conv_wbc: float32 [4, 2, 1024], P(None, None, 'tp'), may hold values from -3 to 3
- dt_bias: float32 [128], P('tp'), may hold values from -3 to 0.5
- a_log: float32 [128], P('tp'), may hold values from -2 to 1.2
- d_skip: float32 [128], P('tp'), may hold values from 0.5 to 1.5
- norm_w: float32 [8192], P('tp'), may hold values from 0.5 to 1.5
- out_w: bfloat16 [8192, 4096], P('tp'), may hold values from -0.0625 to 0.0625
Outputs:
- res_out: bfloat16 [128, 64, 4096], P('rep', None, 'tp')
- slot_out: bfloat16 [96, 64, 4096], P('rep', None, 'tp')
- slot_state: bfloat16 [96, 128, 64, 128], P('rep', 'tp')
The draws below stay inside these ranges and needn't reach their ends.
Inputs may be any that keep to these rules, and one draw needn't show every extreme that they name: `assignment`: request r's handed state starts on replica index r. Each replica receives at most 3 requests and some replica exactly 3. Slot j of a replica serves its j-th request in order of r; inputs of its unused slots are ignored. `res_count`: resident slots j >= the replica's count are spare and give zeros; some replica has exactly 4.
All inputs are finite; a program needn't handle non-finite values.
Results may differ from the reference program's by a relative error of at most 0.019.
Values may be sent and summed in bfloat16 or wider, within the bound.
No kernel may reach another device: no remote copies, remote signals or barrier semaphores. Data moves between devices by JAX's collectives and lax.ppermute only.
A program may use at most 128 MiB of HBM per device.

```python
import jax
import jax.numpy as jnp
from jax import lax

DM = 4096
HEADS = 128
HEAD_DIM = 64
STATE = 128
KERNEL = 4
STEPS = 2
BLOCK = 32
RES = 4
CAP = 3
INNER = 8192
GN = 1024
ROWS = 64
REQUESTS = 32
N_REP = 32


def draw_assignment(key, part):
    key = jax.random.fold_in(key, 11)
    first_key, second_key, third_key = jax.random.split(key, 3)
    busiest = jax.random.randint(first_key, (), 1, N_REP - 1)
    slot_count = N_REP * CAP
    slot_ids = jnp.arange(slot_count)
    owners = slot_ids // CAP
    excluded = (owners == busiest) | (slot_ids == 0) | (slot_ids == (N_REP - 1) * CAP)
    priority = jax.random.permutation(second_key, slot_count) + jnp.where(excluded, slot_count, 0)
    order = jnp.argsort(priority, stable=True)
    chosen = owners[order[:REQUESTS - CAP - 2]].astype(jnp.int32)
    targets = jnp.concatenate([jnp.full((CAP,), busiest, jnp.int32), jnp.zeros((1,), jnp.int32), jnp.full((1,), N_REP - 1, jnp.int32), chosen])
    shuffle = jax.random.permutation(third_key, REQUESTS)
    return targets[shuffle].astype(jnp.int32)


def draw_res_count(key, part):
    key = jax.random.fold_in(key, 7)
    first_key, second_key = jax.random.split(key, 2)
    counts = jax.random.randint(first_key, (N_REP,), 1, RES + 1)
    fullest = jax.random.randint(second_key, (), 0, N_REP)
    return jnp.where(jnp.arange(N_REP) == fullest, RES, counts).astype(jnp.int32)


def shard_levels(rng, shape, pieces, smallest, largest):
    factor_of, own = 1.0, jax.random.fold_in(rng, 6)
    for position, blocks in pieces:
        draws = jnp.exp(jax.random.uniform(jax.random.fold_in(own, position), (blocks,), jnp.float32, smallest / len(pieces), largest / len(pieces)))
        factor_of = factor_of * jnp.repeat(draws, shape[position] // blocks).reshape([-1 if axis == position else 1 for axis in range(len(shape))])
    return factor_of


def centred(rng, dims, spread, most, pieces=(), kind=jnp.bfloat16):
    values = spread * jax.random.normal(rng, dims, jnp.float32)
    if pieces:
        values = values * shard_levels(rng, dims, pieces, -0.22, 0.18)
    return jnp.clip(values, -most, most).astype(kind)


def setup_inputs(seed: int = 0) -> dict:
    key_of = jax.random.split(jax.random.key(seed), 24)
    return {
        "res_state": centred(key_of[0], (N_REP * RES, HEADS, HEAD_DIM, STATE), 0.1, 0.59765625, ((0, 32), (1, 8))),
        "res_conv_x": centred(key_of[1], (N_REP * RES, KERNEL - 1, INNER), 1.0, 6.0, ((0, 32), (2, 8))),
        "res_conv_bc": centred(key_of[2], (N_REP * RES, KERNEL - 1, 2, GN), 1.0, 6.0, ((0, 32), (3, 8))),
        "res_x": centred(key_of[3], (N_REP * RES, ROWS, INNER), 1.0, 6.0, ((0, 32), (2, 8))),
        "res_bc": centred(key_of[4], (N_REP * RES, ROWS, 2, GN), 1.0, 6.0, ((0, 32), (3, 8))),
        "res_z": centred(key_of[5], (N_REP * RES, ROWS, INNER), 1.0, 6.0, ((0, 32), (2, 8))),
        "res_dt": centred(key_of[6], (N_REP * RES, ROWS, HEADS), 0.5, 3.0, ((0, 32), (2, 8))),
        "res_count": draw_res_count(jax.random.fold_in(key_of[23], 71), 0),
        "hand_state": centred(key_of[8], (REQUESTS, HEADS, HEAD_DIM, STATE), 0.1, 0.59765625, ((0, 32), (1, 8))),
        "hand_conv_x": centred(key_of[9], (REQUESTS, KERNEL - 1, INNER), 1.0, 6.0, ((0, 32), (2, 8))),
        "hand_conv_bc": centred(key_of[10], (REQUESTS, KERNEL - 1, 2, GN), 1.0, 6.0, ((0, 32), (3, 8))),
        "slot_x": centred(key_of[11], (N_REP * CAP, ROWS, INNER), 1.0, 6.0, ((0, 32), (2, 8))),
        "slot_bc": centred(key_of[12], (N_REP * CAP, ROWS, 2, GN), 1.0, 6.0, ((0, 32), (3, 8))),
        "slot_z": centred(key_of[13], (N_REP * CAP, ROWS, INNER), 1.0, 6.0, ((0, 32), (2, 8))),
        "slot_dt": centred(key_of[14], (N_REP * CAP, ROWS, HEADS), 0.5, 3.0, ((0, 32), (2, 8))),
        "assignment": draw_assignment(jax.random.fold_in(key_of[23], 71), 0),
        "conv_wx": centred(key_of[16], (KERNEL, INNER), 0.5, 3.0, ((1, 8),), jnp.float32),
        "conv_wbc": centred(key_of[17], (KERNEL, 2, GN), 0.5, 3.0, ((2, 8),), jnp.float32),
        "dt_bias": jnp.clip(-3.0 + 3.5 * jax.random.uniform(key_of[18], (HEADS,), jnp.float32) ** shard_levels(key_of[18], (HEADS,), ((0, 8),), -0.2, 0.2), -3.0, 0.5),
        "a_log": jnp.clip(-2.0 + 3.2 * jax.random.uniform(key_of[19], (HEADS,), jnp.float32) ** shard_levels(key_of[19], (HEADS,), ((0, 8),), -0.2, 0.2), -2.0, 1.2),
        "d_skip": jnp.clip(0.5 + 1.0 * jax.random.uniform(key_of[20], (HEADS,), jnp.float32) ** shard_levels(key_of[20], (HEADS,), ((0, 8),), -0.2, 0.2), 0.5, 1.5),
        "norm_w": jnp.clip(1.0 + 0.1 * jax.random.normal(key_of[21], (INNER,), jnp.float32), 0.5, 1.5),
        "out_w": centred(key_of[22], (INNER, DM), INNER ** -0.5, 0.0625, ((0, 8),)),
    }


def decode_request(hold_state, conv_rows, conv_pairs, input_x, input_pairs, input_gate, input_step, conv_wx, conv_wbc, dt_bias, a_log, d_skip, norm_w, step_count, block_rows):
    head_count, head_dim, width_state = hold_state.shape
    inner_width = conv_rows.shape[-1]
    groups = conv_pairs.shape[-1] // width_state
    per_group = head_count // groups
    kernel = conv_wx.shape[0]
    highest = lax.Precision.HIGHEST
    decay_rate = -jnp.exp(a_log)
    carried = hold_state.astype(jnp.float32)
    positions = jnp.arange(block_rows)
    causal = (positions[:, None] >= positions[None, :])[:, :, None]
    normed_rows = []
    for step_index in range(step_count):
        first_row = step_index * block_rows
        window_x = jnp.concatenate([conv_rows, input_x[first_row:first_row + block_rows]], 0)
        window_pairs = jnp.concatenate([conv_pairs, input_pairs[first_row:first_row + block_rows]], 0)
        conv_rows = window_x[block_rows:]
        conv_pairs = window_pairs[block_rows:]
        summed_x = window_x[0:block_rows].astype(jnp.float32) * conv_wx[0]
        summed_pairs = window_pairs[0:block_rows].astype(jnp.float32) * conv_wbc[0]
        for offset in range(1, kernel):
            summed_x = summed_x + window_x[offset:offset + block_rows].astype(jnp.float32) * conv_wx[offset]
            summed_pairs = summed_pairs + window_pairs[offset:offset + block_rows].astype(jnp.float32) * conv_wbc[offset]
        x_conv = jax.nn.silu(summed_x).reshape(block_rows, groups, per_group, head_dim)
        pairs_conv = jax.nn.silu(summed_pairs)
        coeff_b = pairs_conv[:, 0].reshape(block_rows, groups, width_state)
        coeff_c = pairs_conv[:, 1].reshape(block_rows, groups, width_state)
        step_size = jax.nn.softplus(input_step[first_row:first_row + block_rows].astype(jnp.float32) + dt_bias)
        cum_decay = jnp.cumsum(step_size * decay_rate, axis=0)
        difference = cum_decay[:, None, :] - cum_decay[None, :, :]
        decay_mask = jnp.where(causal, jnp.exp(jnp.where(causal, difference, 0.0)), 0.0)
        scores = jnp.einsum('tgn,sgn->tsg', coeff_c, coeff_b, precision=highest)
        weights = decay_mask.reshape(block_rows, block_rows, groups, per_group) * scores[..., None] * step_size.reshape(1, block_rows, groups, per_group)
        y_inner = jnp.einsum('tsgq,sgqp->tgqp', weights, x_conv, precision=highest)
        grouped = carried.reshape(groups, per_group, head_dim, width_state)
        y_state = jnp.einsum('tgn,gqpn->tgqp', coeff_c, grouped, precision=highest) * jnp.exp(cum_decay).reshape(block_rows, groups, per_group)[..., None]
        output = y_inner + y_state + d_skip.reshape(groups, per_group)[None, :, :, None] * x_conv
        tail_weight = (jnp.exp(cum_decay[-1][None, :] - cum_decay) * step_size).reshape(block_rows, groups, per_group)
        update = jnp.einsum('sgq,sgqp,sgn->gqpn', tail_weight, x_conv, coeff_b, precision=highest)
        carried = carried * jnp.exp(cum_decay[-1])[:, None, None] + update.reshape(head_count, head_dim, width_state)
        gated = output.reshape(block_rows, inner_width) * jax.nn.silu(input_gate[first_row:first_row + block_rows].astype(jnp.float32))
        gated = gated.reshape(block_rows, groups, inner_width // groups)
        mean_square = lax.optimization_barrier(jnp.mean(gated * gated, axis=-1, keepdims=True))
        normed = (gated * lax.rsqrt(mean_square + 1e-05)).reshape(block_rows, inner_width) * norm_w
        normed_rows.append(normed.astype(jnp.bfloat16))
    return (jnp.concatenate(normed_rows, 0), carried.astype(jnp.bfloat16))

def reference(res_state, res_conv_x, res_conv_bc, res_x, res_bc, res_z, res_dt, res_count, hand_state, hand_conv_x, hand_conv_bc, slot_x, slot_bc, slot_z, slot_dt, assignment, conv_wx, conv_wbc, dt_bias, a_log, d_skip, norm_w, out_w):
    params = (conv_wx, conv_wbc, dt_bias, a_log, d_skip, norm_w)

    def run_one(request_item):
        return decode_request(*request_item, *params, STEPS, BLOCK)
    res_normed, _ = lax.map(run_one, (res_state, res_conv_x, res_conv_bc, res_x, res_bc, res_z, res_dt))
    resident_total = res_state.shape[0]
    res_full = jnp.dot(res_normed.reshape(-1, INNER), out_w, preferred_element_type=jnp.float32).reshape(resident_total, ROWS, DM)
    resident_ids = jnp.arange(resident_total)
    live_rows = resident_ids % RES < res_count[resident_ids // RES]
    res_out = jnp.where(live_rows[:, None, None], res_full, 0.0).astype(jnp.bfloat16)
    request_ids = jnp.arange(REQUESTS)
    same_target = assignment[:, None] == assignment[None, :]
    earlier = request_ids[None, :] < request_ids[:, None]
    slot_rank = lax.optimization_barrier(jnp.sum((same_target & earlier).astype(jnp.int32), axis=1)).astype(jnp.int32)
    slot_index = (assignment * CAP + slot_rank).astype(jnp.int32)
    total_slots = N_REP * CAP

    def place_slot(values_array):
        return jnp.zeros((total_slots,) + values_array.shape[1:], values_array.dtype).at[slot_index].set(values_array)
    filled = jnp.zeros((total_slots,), jnp.int32).at[slot_index].set(1)
    slot_valid = filled > 0
    slot_normed, slot_final = lax.map(run_one, (place_slot(hand_state), place_slot(hand_conv_x), place_slot(hand_conv_bc), slot_x, slot_bc, slot_z, slot_dt))
    slot_full = jnp.dot(slot_normed.reshape(-1, INNER), out_w, preferred_element_type=jnp.float32).reshape(total_slots, ROWS, DM)
    slot_out = jnp.where(slot_valid[:, None, None], slot_full, 0.0).astype(jnp.bfloat16)
    slot_state = jnp.where(slot_valid[:, None, None, None], slot_final, jnp.zeros_like(slot_final))
    return (res_out, slot_out, slot_state)
```

```python
import functools

import jax
import jax.numpy as jnp
from jax import lax
from jax.experimental import pallas as pl
from jax.experimental.pallas import tpu as pltpu
from jax.sharding import PartitionSpec as P

F32 = jnp.float32
BF16 = jnp.bfloat16
ROWS = 64
INNER = 1024
STATE = 128
HEADS = 16
PAIRS = HEADS // 2
TAPS = 4
CAP = 3
NX, NZ = 4, 8
NY = 4
TOP = 8
PACK = 1056
HALF = PACK // 2
EARLY = (0, 1, 7, 2, 6)
LATE = (3, 5, 4)
ORDER = EARLY + LATE
VMEM_LIMIT = 48 * 1024 * 1024


def lanes_of(shape):
    return lax.broadcasted_iota(jnp.int32, shape, 1)


def rows_of(shape):
    return lax.broadcasted_iota(jnp.int32, shape, 0)


def mix_rows(win_x, win_bc, dt_pad, gated, dt, z_ref, params, load_state, store_state, out_ref):
    wx, wbc, dt_bias, a_log, d_skip, norm_w = params
    acc = win_bc[TOP - 3 : TOP - 3 + ROWS, :] * wbc[0:1, :]
    for k in range(1, TAPS):
        acc += win_bc[TOP - 3 + k : TOP - 3 + k + ROWS, :] * wbc[k : k + 1, :]
    bcc = acc / (1.0 + jnp.exp(-acc))
    coeff_b = bcc[:, :STATE].astype(BF16)
    coeff_c = bcc[:, STATE:].astype(BF16)

    raw = dt + dt_bias[...]
    step = jnp.maximum(raw, 0.0) + jnp.log(1.0 + jnp.exp(-jnp.abs(raw)))
    dt_pad[...] = jnp.zeros_like(dt_pad)
    dt_pad[0, :, 0:HEADS] = step
    dt_pad[1, :, 0:HEADS] = step * -jnp.exp(a_log[...])
    size = dt_pad[0]
    cum = dt_pad[1]
    row = rows_of((ROWS, 128))
    for shift in (1, 2, 4, 8, 16, 32):
        cum = cum + jnp.where(row >= shift, pltpu.roll(cum, shift, 0), 0.0)

    lane = lanes_of((ROWS, 128))
    left = lane < 64
    source = jnp.where(left, lane, lane - 64)
    causal = row >= source
    diagonal = row == source
    twice_b = jnp.concatenate([coeff_b, coeff_b], axis=0)
    scores = lax.dot_general(
        coeff_c, twice_b, (((1,), (1,)), ((), ())), preferred_element_type=F32
    )
    squares = jnp.zeros((ROWS, 128), F32)
    for pair in range(PAIRS):
        cols = slice(pair * 128, pair * 128 + 128)
        first, second = 2 * pair, 2 * pair + 1

        def spread(values):
            return jnp.where(left, values[:, first : first + 1], values[:, second : second + 1])

        acc = win_x[TOP - 3 : TOP - 3 + ROWS, cols] * wx[0:1, cols]
        for k in range(1, TAPS):
            acc += win_x[TOP - 3 + k : TOP - 3 + k + ROWS, cols] * wx[k : k + 1, cols]
        x_conv = acc / (1.0 + jnp.exp(-acc))
        cum_here = spread(cum)
        x_size = x_conv * spread(size)
        cum_source = jnp.sum(jnp.where(diagonal, cum_here, 0.0), axis=0, keepdims=True)
        decay = jnp.where(causal, jnp.exp(jnp.where(causal, cum_here - cum_source, 0.0)), 0.0)
        weights = (decay * scores).astype(BF16)
        blocks = jnp.concatenate(
            [jnp.where(left, x_size, 0.0), jnp.where(left, 0.0, x_size)], axis=0
        ).astype(BF16)
        y = jnp.dot(weights, blocks, preferred_element_type=F32)
        held = load_state(pair)
        y += jnp.exp(cum_here) * lax.dot_general(
            coeff_c, held, (((1,), (1,)), ((), ())), preferred_element_type=F32
        )
        y += spread(d_skip[...]) * x_conv
        if store_state is not None:
            last = cum_here[ROWS - 1 : ROWS, :]
            tail = (jnp.exp(last - cum_here) * x_size).astype(BF16)
            update = lax.dot_general(
                tail, coeff_b, (((0,), (0,)), ((), ())), preferred_element_type=F32
            )
            final = jnp.exp(cum[ROWS - 1 : ROWS, :])
            keep = jnp.where(
                rows_of((128, 128)) < 64, final[:, first : first + 1], final[:, second : second + 1]
            )
            store_state(pair, held.astype(F32) * keep + update)
        gate = z_ref[0, :, cols].astype(F32)
        g = y * (gate / (1.0 + jnp.exp(-gate)))
        gated[:, cols] = g
        squares += g * g
    scale = lax.rsqrt(jnp.sum(squares, axis=1, keepdims=True) * (1.0 / INNER) + 1e-05)
    out_ref[0] = (gated[...] * scale * norm_w[...]).astype(BF16)


def resident_kernel(
    count, state, conv_x, conv_bc, x, bc, z, dt,
    wx, wbc, dt_bias, a_log, d_skip, norm_w, out, win_x, win_bc, dt_pad, gated,
):
    slot = pl.program_id(0)

    @pl.when(slot < count[0])
    def _():
        win_x[TOP - 3 : TOP, :] = conv_x[0].astype(F32)
        win_x[TOP:, :] = x[0].astype(F32)
        win_bc[TOP - 3 : TOP, :] = conv_bc[0].astype(F32)
        win_bc[TOP:, :] = bc[0].astype(F32)

        def load_state(pair):
            return state[0, 2 * pair : 2 * pair + 2].reshape(128, STATE)

        mix_rows(
            win_x, win_bc, dt_pad, gated, dt[0].astype(F32), z,
            (wx, wbc, dt_bias, a_log, d_skip, norm_w), load_state, None, out,
        )

    @pl.when(slot >= count[0])
    def _():
        out[...] = jnp.zeros_like(out)


ROW_SCRATCH = [
    pltpu.VMEM((TOP + ROWS, INNER), F32),
    pltpu.VMEM((TOP + ROWS, 2 * STATE), F32),
    pltpu.VMEM((2, ROWS, 128), F32),
    pltpu.VMEM((ROWS, INNER), F32),
]


def whole(array):
    return pl.BlockSpec(array.shape, lambda *_: (0,) * array.ndim)


def per_slot(shape):
    return pl.BlockSpec((1,) + shape, lambda i, *_: (i,) + (0,) * len(shape))


def resident_rows(count, state, conv_x, conv_bc, x, bc, z, dt, params):
    slots = state.shape[0]
    return pl.pallas_call(
        resident_kernel,
        grid_spec=pltpu.PrefetchScalarGridSpec(
            num_scalar_prefetch=1,
            grid=(slots,),
            in_specs=[per_slot(a.shape[1:]) for a in (state, conv_x, conv_bc, x, bc, z, dt)]
            + [whole(a) for a in params],
            out_specs=per_slot((ROWS, INNER)),
            scratch_shapes=ROW_SCRATCH,
        ),
        out_shape=jax.ShapeDtypeStruct((slots, ROWS, INNER), BF16),
        compiler_params=pltpu.CompilerParams(vmem_limit_bytes=VMEM_LIMIT),
        cost_estimate=pl.CostEstimate(flops=400_000_000, bytes_accessed=16_000_000, transcendentals=0),
        name="resident_rows",
    )(count, state, conv_x, conv_bc, x, bc, z, dt, *params)


def line_hits(assign, target, column):
    target_z = lax.rem(target, NZ)
    return [
        (assign[column * NZ + lax.rem(target_z + NZ - offset, NZ)] == target).astype(jnp.int32)
        for offset in ORDER
    ]


def round_ranks(hits):
    early = functools.reduce(jnp.maximum, hits[: len(EARLY)])
    ranks, seen = [], jnp.int32(0)
    for hit in hits:
        ranks.append(seen + (1 - early))
        seen = seen + hit
    return ranks


def packet_copies(packets, offset, dst, sem):
    if offset == 4:
        low, high = packets[4]
        return [
            pltpu.make_async_copy(low, dst.at[pl.ds(0, HALF)], sem),
            pltpu.make_async_copy(high, dst.at[pl.ds(HALF, HALF)], sem),
        ]
    return [pltpu.make_async_copy(packets[offset], dst, sem)]


def forward_kernel(rounds, offsets, info, *refs):
    count = len(offsets) + (1 if 4 in offsets else 0)
    ins, outs, sems = refs[:count], refs[count:-1], refs[-1]
    packets, at = {}, 0
    for offset in offsets:
        if offset == 4:
            packets[4] = (ins[at], ins[at + 1])
            at += 2
        else:
            packets[offset] = ins[at]
            at += 1
    me = info[32]
    column, z = lax.div(me, NZ), lax.rem(me, NZ)
    todo = []
    for shift in range(1, NX):
        target = lax.rem(column + shift, NX) * NZ + z
        hits = line_hits(info, target, column)
        ranks = round_ranks(hits)
        for n, wanted in enumerate(rounds):
            slot = n * (NX - 1) + shift - 1
            for offset, hit, rank in zip(ORDER, hits, ranks):
                if offset in packets:
                    todo.append(
                        ((hit == 1) & (rank == wanted),
                         packet_copies(packets, offset, outs[slot], sems.at[slot]))
                    )
    for wanted, copies in todo:
        @pl.when(wanted)
        def _(copies=copies):
            for copy in copies:
                copy.start()
    for wanted, copies in todo:
        @pl.when(wanted)
        def _(copies=copies):
            for copy in copies:
                copy.wait()


def forward(rounds, offsets, info, packets):
    count = len(rounds) * (NX - 1)
    return pl.pallas_call(
        functools.partial(forward_kernel, rounds, offsets),
        in_specs=[pl.BlockSpec(memory_space=pltpu.SMEM)]
        + [pl.BlockSpec(memory_space=pl.ANY)] * len(packets),
        out_specs=[pl.BlockSpec(memory_space=pl.ANY)] * count,
        out_shape=[jax.ShapeDtypeStruct((PACK, 128), BF16)] * count,
        scratch_shapes=[pltpu.SemaphoreType.DMA((count,))],
        cost_estimate=pl.CostEstimate(flops=0, bytes_accessed=3_000_000, transcendentals=0),
        name="forward",
    )(info, *packets)


def blank_kernel(info, *outs):
    pass


def blank(info, count):
    return pl.pallas_call(
        blank_kernel,
        in_specs=[pl.BlockSpec(memory_space=pltpu.SMEM)],
        out_specs=[pl.BlockSpec(memory_space=pl.ANY)] * count,
        out_shape=[jax.ShapeDtypeStruct((PACK, 128), BF16)] * count,
        name="blank",
    )(info)


PACKETS = 9
ARRIVED = 4 * (NX - 1)


def slot_kernel(info, *refs):
    line, rest = refs[:PACKETS], refs[PACKETS:]
    came, rest = rest[:ARRIVED], rest[ARRIVED:]
    (x, bc, z, dt, wx, wbc, dt_bias, a_log, d_skip, norm_w, out, state,
     held, valid, win_x, win_bc, dt_pad, gated, sems) = rest
    packets = {o: line[i] for i, o in enumerate(ORDER[:-1])}
    packets[4] = (line[PACKETS - 2], line[PACKETS - 1])
    slot = pl.program_id(0)
    me = info[32]
    column, my_z = lax.div(me, NZ), lax.rem(me, NZ)

    @pl.when(slot == 0)
    def _():
        before = jnp.int32(0)
        order = []
        for request in range(NX * NZ):
            mine = (info[request] == me).astype(jnp.int32)
            order.append(before)
            before = before + mine
        valid[0] = before
        for shift in range(NX):
            sender = lax.rem(column + NX - shift, NX)
            hits = line_hits(info, me, sender)
            ranks = round_ranks(hits)
            for offset, hit, rank in zip(ORDER, hits, ranks):
                source = sender * NZ + lax.rem(my_z + NZ - offset, NZ)
                place = jnp.int32(0)
                for request in range(NX * NZ):
                    place = jnp.where(source == request, order[request], place)

                @pl.when(hit == 1)
                def _(shift=shift, offset=offset, rank=rank, place=place):
                    if shift == 0:
                        for copy in packet_copies(packets, offset, held.at[place], sems.at[place]):
                            copy.start()
                    else:
                        for n in range(4):
                            @pl.when(rank == n)
                            def _(n=n):
                                pltpu.make_async_copy(
                                    came[n * (NX - 1) + shift - 1], held.at[place], sems.at[place]
                                ).start()

    live = slot < valid[0]

    @pl.when(live)
    def _():
        win_x[TOP:, :] = x[0].astype(F32)
        win_bc[TOP:, :] = bc[0].astype(F32)
        pltpu.make_async_copy(held.at[slot], held.at[slot], sems.at[slot]).wait()
        conv = held[slot, 1024:PACK, :].astype(F32)
        for k in range(TAPS - 1):
            for b in range(8):
                win_x[TOP - 3 + k : TOP - 2 + k, 128 * b : 128 * b + 128] = conv[
                    8 * k + b : 8 * k + b + 1
                ]
            for b in range(2):
                win_bc[TOP - 3 + k : TOP - 2 + k, 128 * b : 128 * b + 128] = conv[
                    24 + 2 * k + b : 25 + 2 * k + b
                ]

        def load_state(pair):
            return held[slot, 128 * pair : 128 * pair + 128, :]

        def store_state(pair, value):
            state[0, 2 * pair : 2 * pair + 2] = value.astype(BF16).reshape(2, 64, STATE)

        mix_rows(
            win_x, win_bc, dt_pad, gated, dt[0].astype(F32), z,
            (wx, wbc, dt_bias, a_log, d_skip, norm_w), load_state, store_state, out,
        )

    @pl.when(jnp.logical_not(live))
    def _():
        out[...] = jnp.zeros_like(out)
        state[...] = jnp.zeros_like(state)


def slot_rows(info, line, came, x, bc, z, dt, params):
    slots = x.shape[0]
    return pl.pallas_call(
        slot_kernel,
        grid=(slots,),
        in_specs=[pl.BlockSpec(memory_space=pltpu.SMEM)]
        + [pl.BlockSpec(memory_space=pl.ANY)] * (PACKETS + ARRIVED)
        + [per_slot(a.shape[1:]) for a in (x, bc, z, dt)]
        + [whole(a) for a in params],
        out_specs=[per_slot((ROWS, INNER)), per_slot((HEADS, 64, STATE))],
        out_shape=[
            jax.ShapeDtypeStruct((slots, ROWS, INNER), BF16),
            jax.ShapeDtypeStruct((slots, HEADS, 64, STATE), BF16),
        ],
        scratch_shapes=[pltpu.VMEM((CAP, PACK, 128), BF16), pltpu.SMEM((1,), jnp.int32)]
        + ROW_SCRATCH
        + [pltpu.SemaphoreType.DMA((CAP,))],
        compiler_params=pltpu.CompilerParams(vmem_limit_bytes=VMEM_LIMIT),
        cost_estimate=pl.CostEstimate(flops=400_000_000, bytes_accessed=20_000_000, transcendentals=0),
        name="slot_rows",
    )(info, *line, *came, x, bc, z, dt, *params)


def project_kernel(blocks, rows, weight, out):
    out[0] = jnp.dot(rows[...], weight[...], preferred_element_type=F32).astype(BF16)


def project(blocks, rows, weight):
    count, width = blocks.shape[0], weight.shape[1] // 8
    return pl.pallas_call(
        project_kernel,
        grid_spec=pltpu.PrefetchScalarGridSpec(
            num_scalar_prefetch=1,
            grid=(count,),
            in_specs=[
                pl.BlockSpec(rows.shape, lambda i, blocks: (0, 0)),
                pl.BlockSpec((weight.shape[0], width), lambda i, blocks: (0, blocks[i])),
            ],
            out_specs=pl.BlockSpec((1, rows.shape[0], width), lambda i, blocks: (i, 0, 0)),
        ),
        out_shape=jax.ShapeDtypeStruct((count, rows.shape[0], width), BF16),
        compiler_params=pltpu.CompilerParams(vmem_limit_bytes=VMEM_LIMIT),
        cost_estimate=pl.CostEstimate(
            flops=2 * count * rows.shape[0] * weight.shape[0] * width,
            bytes_accessed=6_000_000, transcendentals=0,
        ),
        name="project",
    )(blocks, rows, weight)


def reduce_out(normed, out_w, sent, kept):
    slots = normed.shape[0]
    rows = normed.reshape(slots * ROWS, INNER)
    mates = [(t, t ^ 1) for t in range(2 * NY)]
    from_mate = lax.ppermute(project(sent, rows, out_w), "tp", mates)
    own = project(kept, rows, out_w)
    chip = [own[k].astype(F32) + from_mate[k].astype(F32) for k in range(NY)]
    total = chip[0]
    for k in range(1, NY):
        shifted = [(t, (t + 2 * k) % (2 * NY)) for t in range(2 * NY)]
        total = total + lax.ppermute(chip[k].astype(BF16), "tp", shifted).astype(F32)
    return total.astype(BF16).reshape(slots, ROWS, -1)


def along_z(array, step):
    pairs = [(x * NZ + z, x * NZ + (z + step) % NZ) for x in range(NX) for z in range(NZ)]
    return lax.ppermute(array, "rep", pairs)


def along_x(arrays):
    return [
        lax.ppermute(
            array, "rep",
            [(x * NZ + z, (x + shift) % NX * NZ + z) for x in range(NX) for z in range(NZ)],
        )
        for shift, array in zip([1, 2, 3] * 4, arrays)
    ]


def on_device(
    res_state, res_conv_x, res_conv_bc, res_x, res_bc, res_z, res_dt, res_count,
    hand_state, hand_conv_x, hand_conv_bc, slot_x, slot_bc, slot_z, slot_dt,
    assignment, conv_wx, conv_wbc, dt_bias, a_log, d_skip, norm_w, out_w,
):
    me = lax.axis_index("rep")
    tp = lax.axis_index("tp")
    info = jnp.concatenate([assignment, me[None].astype(jnp.int32)])
    packet = jnp.concatenate(
        [
            hand_state.reshape(-1, STATE),
            hand_conv_x.reshape(-1, STATE),
            hand_conv_bc.reshape(-1, STATE),
            jnp.zeros((2, STATE), BF16),
        ],
        axis=0,
    )
    up1, down1 = along_z(packet, 1), along_z(packet, -1)
    up2, down2 = along_z(packet, 2), along_z(packet, -2)

    params = (
        conv_wx, conv_wbc.reshape(TAPS, 2 * STATE), dt_bias[None], a_log[None], d_skip[None],
        norm_w[None],
    )
    res_normed = resident_rows(
        res_count, res_state, res_conv_x, res_conv_bc.reshape(-1, TAPS - 1, 2 * STATE), res_x,
        res_bc.reshape(-1, ROWS, 2 * STATE), res_z, res_dt, params,
    )
    chip, core = tp // 2, tp % 2
    turns = (chip + jnp.arange(NY, dtype=jnp.int32)) % NY
    sent, kept = 2 * turns + 1 - core, 2 * turns + core

    early = [packet, up1, down1, up2, down2]
    first = along_x(forward((0,), EARLY, info, early))
    up3, down3 = along_z(up2, 1), along_z(down2, -1)
    up4, down4 = along_z(up2[:HALF], 2), along_z(down2[HALF:], -2)
    line = early + [up3, down3, up4, down4]
    res_out = reduce_out(res_normed, out_w, sent, kept)
    second = along_x(forward((1,), ORDER, info, line))

    ids = jnp.arange(NX * NZ)
    goes = assignment[None, :] == ids[:, None]
    offset = (ids[:, None] - ids[None, :]) % NZ
    far = (offset > 2) & (offset < 6)
    all_hits = jnp.sum(goes.reshape(-1, NX, NZ), axis=2)
    near_hits = jnp.sum((goes & ~far).reshape(-1, NX, NZ), axis=2)
    across = (ids[:, None] // NZ) != jnp.arange(NX)[None, :]
    more = jnp.any(across & (all_hits - jnp.minimum(near_hits, 1) > 1))
    third = lax.cond(
        more,
        lambda *held: tuple(along_x(forward((2, 3), ORDER, held[0], held[1:]))),
        lambda *held: tuple(blank(held[0], 2 * (NX - 1))),
        info, *line,
    )
    slot_normed, slot_state = slot_rows(
        info, line, first + second + list(third), slot_x,
        slot_bc.reshape(-1, ROWS, 2 * STATE), slot_z, slot_dt, params,
    )
    slot_out = reduce_out(slot_normed, out_w, sent, kept)
    return res_out, slot_out, slot_state


def solution(mesh):
    rows = P("rep", None, "tp")
    pairs = P("rep", None, None, "tp")
    states = P("rep", "tp", None, None)
    return jax.shard_map(
        on_device,
        mesh=mesh,
        in_specs=(
            states, rows, pairs, rows, pairs, rows, rows, P("rep"),
            states, rows, pairs, rows, pairs, rows, rows,
            P(), P(None, "tp"), P(None, None, "tp"), P("tp"), P("tp"), P("tp"), P("tp"),
            P("tp", None),
        ),
        out_specs=(rows, rows, states),
        check_vma=False,
    )
```

```python
import functools

import jax
import jax.numpy as jnp
from jax import lax
from jax.experimental import pallas as pl
from jax.experimental.pallas import tpu as pltpu
from jax.sharding import PartitionSpec as P

F32 = jnp.float32
BF16 = jnp.bfloat16
ROWS = 64
INNER = 1024
STATE = 128
HEADS = 16
PAIRS = HEADS // 2
TAPS = 4
CAP = 3
NX, NZ = 4, 8
NY = 4
TOP = 8
PACK = 1056
HALF = PACK // 2
EARLY = (0, 1, 7, 2, 6)
LATE = (3, 5, 4)
ORDER = EARLY + LATE
VMEM_LIMIT = 58 * 1024 * 1024


def lanes_of(shape):
    return lax.broadcasted_iota(jnp.int32, shape, 1)


def rows_of(shape):
    return lax.broadcasted_iota(jnp.int32, shape, 0)


def mix_rows(win_x, win_bc, dt_pad, gated, dt, z_ref, params, load_state, store_state, normed, slot):
    wx, wbc, dt_bias, a_log, d_skip, norm_w = params
    coeffs = []
    for part in range(2):
        cols = slice(part * STATE, part * STATE + STATE)
        acc = win_bc[TOP - 3 : TOP - 3 + ROWS, cols] * wbc[0, part : part + 1, :]
        for k in range(1, TAPS):
            acc += win_bc[TOP - 3 + k : TOP - 3 + k + ROWS, cols] * wbc[k, part : part + 1, :]
        coeffs.append((acc / (1.0 + jnp.exp(-acc))).astype(BF16))
    coeff_b, coeff_c = coeffs

    dt_pad[...] = jnp.zeros_like(dt_pad)
    dt_pad[0:HEADS, 0:ROWS] = dt[0].astype(F32)
    raw = dt_pad[...].T[0:ROWS, 0:HEADS] + dt_bias[...]
    step = jnp.maximum(raw, 0.0) + jnp.log(1.0 + jnp.exp(-jnp.abs(raw)))
    dt_pad[...] = jnp.zeros_like(dt_pad)
    dt_pad[0:ROWS, 0:HEADS] = step
    dt_pad[ROWS:, 0:HEADS] = step * -jnp.exp(a_log[...])
    size = dt_pad[0:ROWS]
    cum = dt_pad[ROWS:]
    row = rows_of((ROWS, 128))
    for shift in (1, 2, 4, 8, 16, 32):
        cum = cum + jnp.where(row >= shift, pltpu.roll(cum, shift, 0), 0.0)

    lane = lanes_of((ROWS, 128))
    left = lane < 64
    source = jnp.where(left, lane, lane - 64)
    causal = row >= source
    diagonal = row == source
    twice_b = jnp.concatenate([coeff_b, coeff_b], axis=0)
    scores = lax.dot_general(
        coeff_c, twice_b, (((1,), (1,)), ((), ())), preferred_element_type=F32
    )
    squares = jnp.zeros((ROWS, 128), F32)
    for pair in range(PAIRS):
        cols = slice(pair * 128, pair * 128 + 128)
        first, second = 2 * pair, 2 * pair + 1

        def spread(values):
            return jnp.where(left, values[:, first : first + 1], values[:, second : second + 1])

        acc = win_x[TOP - 3 : TOP - 3 + ROWS, cols] * wx[0:1, cols]
        for k in range(1, TAPS):
            acc += win_x[TOP - 3 + k : TOP - 3 + k + ROWS, cols] * wx[k : k + 1, cols]
        x_conv = acc / (1.0 + jnp.exp(-acc))
        cum_here = spread(cum)
        x_size = x_conv * spread(size)
        cum_source = jnp.sum(jnp.where(diagonal, cum_here, 0.0), axis=0, keepdims=True)
        decay = jnp.where(causal, jnp.exp(jnp.where(causal, cum_here - cum_source, 0.0)), 0.0)
        weights = (decay * scores).astype(BF16)
        blocks = jnp.concatenate(
            [jnp.where(left, x_size, 0.0), jnp.where(left, 0.0, x_size)], axis=0
        ).astype(BF16)
        y = jnp.dot(weights, blocks, preferred_element_type=F32)
        held = load_state(pair)
        y += jnp.exp(cum_here) * lax.dot_general(
            coeff_c, held, (((1,), (1,)), ((), ())), preferred_element_type=F32
        )
        y += spread(d_skip[...]) * x_conv
        if store_state is not None:
            last = cum_here[ROWS - 1 : ROWS, :]
            tail = (jnp.exp(last - cum_here) * x_size).astype(BF16)
            update = lax.dot_general(
                tail, coeff_b, (((0,), (0,)), ((), ())), preferred_element_type=F32
            )
            final = jnp.exp(cum[ROWS - 1 : ROWS, :])
            keep = jnp.where(
                rows_of((128, 128)) < 64, final[:, first : first + 1], final[:, second : second + 1]
            )
            store_state(pair, held.astype(F32) * keep + update)
        gate = z_ref[0, :, cols].astype(F32)
        g = y * (gate / (1.0 + jnp.exp(-gate)))
        gated[:, cols] = g
        squares += g * g
    scale = lax.rsqrt(jnp.sum(squares, axis=1, keepdims=True) * (1.0 / INNER) + 1e-05)
    normed[pl.ds(slot * ROWS, ROWS), :] = (gated[...] * scale * norm_w[...]).astype(BF16)


def load_pairs(win_bc, bc):
    both = bc[0].astype(F32)
    win_bc[TOP:, :STATE] = both[:, 0, :]
    win_bc[TOP:, STATE:] = both[:, 1, :]


def project(blocks, normed, weight, sent, kept):
    width = sent.shape[2]
    for at, out in ((0, sent), (NY, kept)):
        for k in range(NY):
            start = pl.multiple_of(blocks[at + k] * width, width)
            out[k] = jnp.dot(
                normed[...], weight[:, pl.ds(start, width)], preferred_element_type=F32
            ).astype(BF16)


def resident_kernel(
    count, blocks, out_w, state, conv_x, conv_bc, x, bc, z, dt,
    wx, wbc, dt_bias, a_log, d_skip, norm_w, sent, kept, conv_rows, normed, weight,
    weight_sem, win_x, win_bc, dt_pad, gated,
):
    slot = pl.program_id(0)
    fetch = pltpu.make_async_copy(out_w, weight, weight_sem)

    @pl.when(slot == 0)
    def _():
        fetch.start()
        conv_rows[...] = conv_x[...].astype(F32)

    @pl.when(slot < count[0])
    def _():
        for k in range(TAPS - 1):
            win_x[TOP - 3 + k : TOP - 2 + k, :] = conv_rows[k, pl.ds(slot, 1), :]
        win_x[TOP:, :] = x[0].astype(F32)
        for k in range(TAPS - 1):
            both = conv_bc[0, k].astype(F32)
            for part in range(2):
                win_bc[TOP - 3 + k : TOP - 2 + k, part * STATE : part * STATE + STATE] = both[
                    part : part + 1
                ]
        load_pairs(win_bc, bc)

        def load_state(pair):
            return state[0, 2 * pair : 2 * pair + 2].reshape(128, STATE)

        mix_rows(
            win_x, win_bc, dt_pad, gated, dt, z,
            (wx, wbc, dt_bias, a_log, d_skip, norm_w), load_state, None, normed, slot,
        )

    @pl.when(slot >= count[0])
    def _():
        normed[pl.ds(slot * ROWS, ROWS), :] = jnp.zeros((ROWS, INNER), BF16)

    @pl.when(slot == pl.num_programs(0) - 1)
    def _():
        fetch.wait()
        project(blocks, normed, weight, sent, kept)


ROW_SCRATCH = [
    pltpu.VMEM((TOP + ROWS, INNER), F32),
    pltpu.VMEM((TOP + ROWS, 2 * STATE), F32),
    pltpu.VMEM((2 * ROWS, 128), F32),
    pltpu.VMEM((ROWS, INNER), F32),
]


def whole(array):
    return pl.BlockSpec(array.shape, lambda *_: (0,) * array.ndim)


def per_slot(shape):
    return pl.BlockSpec((1,) + shape, lambda i, *_: (i,) + (0,) * len(shape))


def row_scratch(slots):
    return [
        pltpu.VMEM((slots * ROWS, INNER), BF16),
        pltpu.VMEM((INNER, 4096), BF16),
        pltpu.SemaphoreType.DMA,
    ] + ROW_SCRATCH


def partial_sums(slots):
    shape = (NY, slots * ROWS, 4096 // 8)
    return [jax.ShapeDtypeStruct(shape, BF16)] * 2


def resident_rows(count, blocks, out_w, state, conv_x, conv_bc, x, bc, z, dt, params):
    slots = state.shape[0]
    sums = partial_sums(slots)
    return pl.pallas_call(
        resident_kernel,
        grid=(slots,),
        in_specs=[pl.BlockSpec(memory_space=pltpu.SMEM)] * 2
        + [pl.BlockSpec(memory_space=pl.ANY), per_slot(state.shape[1:]), whole(conv_x)]
        + [per_slot(a.shape[1:]) for a in (conv_bc, x, bc, z, dt)]
        + [whole(a) for a in params],
        out_specs=[whole(a) for a in sums],
        out_shape=sums,
        scratch_shapes=[pltpu.VMEM((TAPS - 1, slots, INNER), F32)] + row_scratch(slots),
        compiler_params=pltpu.CompilerParams(vmem_limit_bytes=VMEM_LIMIT),
        cost_estimate=pl.CostEstimate(
            flops=3_000_000_000, bytes_accessed=16_000_000, transcendentals=0
        ),
        name="resident_rows",
    )(count, blocks, out_w, state, conv_x, conv_bc, x, bc, z, dt, *params)


def line_hits(assign, target, column):
    target_z = lax.rem(target, NZ)
    return [
        (assign[column * NZ + lax.rem(target_z + NZ - offset, NZ)] == target).astype(jnp.int32)
        for offset in ORDER
    ]


def round_ranks(hits):
    early = functools.reduce(jnp.maximum, hits[: len(EARLY)])
    ranks, seen = [], jnp.int32(0)
    for hit in hits:
        ranks.append(seen + (1 - early))
        seen = seen + hit
    return ranks


def packet_copies(packets, offset, dst, sem):
    if offset == 4:
        low, high = packets[4]
        return [
            pltpu.make_async_copy(low, dst.at[pl.ds(0, HALF)], sem),
            pltpu.make_async_copy(high, dst.at[pl.ds(HALF, HALF)], sem),
        ]
    return [pltpu.make_async_copy(packets[offset], dst, sem)]


def forward_kernel(rounds, offsets, info, *refs):
    count = len(offsets) + (1 if 4 in offsets else 0)
    ins, outs, sems = refs[:count], refs[count:-1], refs[-1]
    halves = []
    if 4 not in offsets:
        halves = [
            pltpu.make_async_copy(
                ins[offsets.index(2)].at[pl.ds(0, HALF)], outs[-2], sems.at[NX - 1]
            ),
            pltpu.make_async_copy(
                ins[offsets.index(6)].at[pl.ds(HALF, HALF)], outs[-1], sems.at[NX]
            ),
        ]
    for copy in halves:
        copy.start()
    packets, at = {}, 0
    for offset in offsets:
        if offset == 4:
            packets[4] = (ins[at], ins[at + 1])
            at += 2
        else:
            packets[offset] = ins[at]
            at += 1
    me = info[32]
    column, z = lax.div(me, NZ), lax.rem(me, NZ)
    todo = []
    for shift in range(1, NX):
        target = lax.rem(column + shift, NX) * NZ + z
        hits = line_hits(info, target, column)
        ranks = round_ranks(hits)
        for n, wanted in enumerate(rounds):
            slot = n * (NX - 1) + shift - 1
            for offset, hit, rank in zip(ORDER, hits, ranks):
                if offset in packets:
                    todo.append(
                        ((hit == 1) & (rank == wanted),
                         packet_copies(packets, offset, outs[slot], sems.at[slot]))
                    )
    for wanted, copies in todo:
        @pl.when(wanted)
        def _(copies=copies):
            for copy in copies:
                copy.start()
    for wanted, copies in todo:
        @pl.when(wanted)
        def _(copies=copies):
            for copy in copies:
                copy.wait()
    for copy in halves:
        copy.wait()


def forward(rounds, offsets, info, packets):
    count = len(rounds) * (NX - 1)
    shapes = [(PACK, 128)] * count + ([] if 4 in offsets else [(HALF, 128)] * 2)
    return pl.pallas_call(
        functools.partial(forward_kernel, rounds, offsets),
        in_specs=[pl.BlockSpec(memory_space=pltpu.SMEM)]
        + [pl.BlockSpec(memory_space=pl.ANY)] * len(packets),
        out_specs=[pl.BlockSpec(memory_space=pl.ANY)] * len(shapes),
        out_shape=[jax.ShapeDtypeStruct(shape, BF16) for shape in shapes],
        scratch_shapes=[pltpu.SemaphoreType.DMA((len(shapes),))],
        cost_estimate=pl.CostEstimate(flops=0, bytes_accessed=3_000_000, transcendentals=0),
        name="forward",
    )(info, *packets)


def blank_kernel(info, *outs):
    pass


def blank(info, count):
    return pl.pallas_call(
        blank_kernel,
        in_specs=[pl.BlockSpec(memory_space=pltpu.SMEM)],
        out_specs=[pl.BlockSpec(memory_space=pl.ANY)] * count,
        out_shape=[jax.ShapeDtypeStruct((PACK, 128), BF16)] * count,
        name="blank",
    )(info)


PACKETS = 9
ARRIVED = 4 * (NX - 1)


def slot_kernel(info, blocks, out_w, *refs):
    line, rest = refs[:PACKETS], refs[PACKETS:]
    came, rest = rest[:ARRIVED], rest[ARRIVED:]
    (x, bc, z, dt, wx, wbc, dt_bias, a_log, d_skip, norm_w, sent, kept, state,
     held, valid, sems, normed, weight, weight_sem, win_x, win_bc, dt_pad, gated) = rest
    fetch = pltpu.make_async_copy(out_w, weight, weight_sem)
    packets = {o: line[i] for i, o in enumerate(ORDER[:-1])}
    packets[4] = (line[PACKETS - 2], line[PACKETS - 1])
    slot = pl.program_id(0)
    me = info[32]
    column, my_z = lax.div(me, NZ), lax.rem(me, NZ)

    @pl.when(slot == 0)
    def _():
        before = jnp.int32(0)
        for request in range(NX * NZ):
            valid[request] = before
            before = before + (info[request] == me).astype(jnp.int32)
        valid[NX * NZ] = before
        for shift in range(NX):
            sender = lax.rem(column + NX - shift, NX)
            hits = line_hits(info, me, sender)
            ranks = round_ranks(hits)
            for offset, hit, rank in zip(ORDER, hits, ranks):
                source = sender * NZ + lax.rem(my_z + NZ - offset, NZ)
                place = valid[source]

                @pl.when(hit == 1)
                def _(shift=shift, offset=offset, rank=rank, place=place):
                    if shift == 0:
                        for copy in packet_copies(packets, offset, held.at[place], sems.at[place]):
                            copy.start()
                    else:
                        for n in range(4):
                            @pl.when(rank == n)
                            def _(n=n):
                                pltpu.make_async_copy(
                                    came[n * (NX - 1) + shift - 1], held.at[place], sems.at[place]
                                ).start()
        fetch.start()

    live = slot < valid[NX * NZ]

    @pl.when(live)
    def _():
        win_x[TOP:, :] = x[0].astype(F32)
        load_pairs(win_bc, bc)
        pltpu.make_async_copy(held.at[slot], held.at[slot], sems.at[slot]).wait()
        conv = held[slot, 1024:PACK, :].astype(F32)
        for k in range(TAPS - 1):
            for b in range(8):
                win_x[TOP - 3 + k : TOP - 2 + k, 128 * b : 128 * b + 128] = conv[
                    8 * k + b : 8 * k + b + 1
                ]
            for b in range(2):
                win_bc[TOP - 3 + k : TOP - 2 + k, 128 * b : 128 * b + 128] = conv[
                    24 + 2 * k + b : 25 + 2 * k + b
                ]

        def load_state(pair):
            return held[slot, 128 * pair : 128 * pair + 128, :]

        def store_state(pair, value):
            state[0, 2 * pair : 2 * pair + 2] = value.astype(BF16).reshape(2, 64, STATE)

        mix_rows(
            win_x, win_bc, dt_pad, gated, dt, z,
            (wx, wbc, dt_bias, a_log, d_skip, norm_w), load_state, store_state, normed, slot,
        )

    @pl.when(jnp.logical_not(live))
    def _():
        normed[pl.ds(slot * ROWS, ROWS), :] = jnp.zeros((ROWS, INNER), BF16)
        state[...] = jnp.zeros_like(state)

    @pl.when(slot == pl.num_programs(0) - 1)
    def _():
        fetch.wait()
        project(blocks, normed, weight, sent, kept)


def slot_rows(info, blocks, out_w, line, came, x, bc, z, dt, params):
    slots = x.shape[0]
    sums = partial_sums(slots)
    return pl.pallas_call(
        slot_kernel,
        grid=(slots,),
        in_specs=[pl.BlockSpec(memory_space=pltpu.SMEM)] * 2
        + [pl.BlockSpec(memory_space=pl.ANY)] * (1 + PACKETS + ARRIVED)
        + [per_slot(a.shape[1:]) for a in (x, bc, z, dt)]
        + [whole(a) for a in params],
        out_specs=[whole(a) for a in sums] + [per_slot((HEADS, 64, STATE))],
        out_shape=sums + [jax.ShapeDtypeStruct((slots, HEADS, 64, STATE), BF16)],
        scratch_shapes=[
            pltpu.VMEM((CAP, PACK, 128), BF16),
            pltpu.SMEM((NX * NZ + 1,), jnp.int32),
            pltpu.SemaphoreType.DMA((CAP,)),
        ]
        + row_scratch(slots),
        compiler_params=pltpu.CompilerParams(vmem_limit_bytes=VMEM_LIMIT),
        cost_estimate=pl.CostEstimate(
            flops=3_000_000_000, bytes_accessed=20_000_000, transcendentals=0
        ),
        name="slot_rows",
    )(info, blocks, out_w, *line, *came, x, bc, z, dt, *params)


def across_cores(array):
    return lax.ppermute(array, "tp", [(t, t ^ 1) for t in range(2 * NY)])


def chip_sums(own, from_mate):
    return [own[k].astype(F32) + from_mate[k].astype(F32) for k in range(NY)]


def reduce_out(chip, slots):
    total = chip[0]
    for k in range(1, NY):
        shifted = [(t, (t + 2 * k) % (2 * NY)) for t in range(2 * NY)]
        total = total + lax.ppermute(chip[k].astype(BF16), "tp", shifted).astype(F32)
    return total.astype(BF16).reshape(slots, ROWS, -1)


def along_z(array, step):
    pairs = [(x * NZ + z, x * NZ + (z + step) % NZ) for x in range(NX) for z in range(NZ)]
    return lax.ppermute(array, "rep", pairs)


def along_x(arrays):
    return [
        lax.ppermute(
            array, "rep",
            [(x * NZ + z, (x + shift) % NX * NZ + z) for x in range(NX) for z in range(NZ)],
        )
        for shift, array in zip([1, 2, 3] * 4, arrays)
    ]


def on_device(
    res_state, res_conv_x, res_conv_bc, res_x, res_bc, res_z, res_dt, res_count,
    hand_state, hand_conv_x, hand_conv_bc, slot_x, slot_bc, slot_z, slot_dt,
    assignment, conv_wx, conv_wbc, dt_bias, a_log, d_skip, norm_w, out_w,
):
    me = lax.axis_index("rep")
    tp = lax.axis_index("tp")
    info = jnp.concatenate([assignment, me[None].astype(jnp.int32)])
    packet = jnp.concatenate(
        [
            hand_state.reshape(-1, STATE),
            hand_conv_x.reshape(-1, STATE),
            hand_conv_bc.reshape(-1, STATE),
            jnp.zeros((2, STATE), BF16),
        ],
        axis=0,
    )
    up1, down1 = along_z(packet, 1), along_z(packet, -1)
    up2, down2 = along_z(packet, 2), along_z(packet, -2)

    params = (
        conv_wx, conv_wbc, dt_bias[None], a_log[None], d_skip[None],
        norm_w[None],
    )
    chip, core = tp // 2, tp % 2
    turns = (chip + jnp.arange(NY, dtype=jnp.int32)) % NY
    blocks = jnp.concatenate([2 * turns + 1 - core, 2 * turns + core])
    res_sent, res_kept = resident_rows(
        res_count, blocks, out_w, res_state, res_conv_x.transpose(1, 0, 2),
        res_conv_bc, res_x, res_bc, res_z, res_dt.transpose(0, 2, 1), params,
    )
    up1, down1, up2, down2, res_sent, res_kept = lax.optimization_barrier(
        (up1, down1, up2, down2, res_sent, res_kept)
    )

    early = [packet, up1, down1, up2, down2]
    *ahead, up2_half, down2_half = forward((0,), EARLY, info, early)
    up4, down4 = along_z(up2_half, 2), along_z(down2_half, -2)
    up3, down3 = along_z(up2, 1), along_z(down2, -1)
    first = along_x(ahead)
    res_mate = across_cores(res_sent)
    up3, down3, up4, down4, *first = lax.optimization_barrier((up3, down3, up4, down4, *first))
    line = early + [up3, down3, up4, down4]
    ahead = forward((1,), ORDER, info, line)
    *ahead, info, res_mate, res_kept = lax.optimization_barrier((*ahead, info, res_mate, res_kept))
    second = along_x(ahead)
    res_chip = chip_sums(res_kept, res_mate)

    ids = jnp.arange(NX * NZ)
    goes = assignment[None, :] == ids[:, None]
    offset = (ids[:, None] - ids[None, :]) % NZ
    far = (offset > 2) & (offset < 6)
    all_hits = jnp.sum(goes.reshape(-1, NX, NZ), axis=2)
    near_hits = jnp.sum((goes & ~far).reshape(-1, NX, NZ), axis=2)
    across = (ids[:, None] // NZ) != jnp.arange(NX)[None, :]
    more = jnp.any(across & (all_hits - jnp.minimum(near_hits, 1) > 1))
    third = lax.cond(
        more,
        lambda *held: tuple(along_x(forward((2, 3), ORDER, held[0], held[1:]))),
        lambda *held: tuple(blank(held[0], 2 * (NX - 1))),
        info, *line,
    )
    res_out = reduce_out(res_chip, res_state.shape[0])
    *second, res_out = lax.optimization_barrier((*second, res_out))
    sent, kept, slot_state = slot_rows(
        info, blocks, out_w, line, first + second + list(third), slot_x, slot_bc, slot_z,
        slot_dt.transpose(0, 2, 1), params,
    )
    slot_out = reduce_out(chip_sums(kept, across_cores(sent)), slot_x.shape[0])
    return res_out, slot_out, slot_state


def solution(mesh):
    rows = P("rep", None, "tp")
    pairs = P("rep", None, None, "tp")
    states = P("rep", "tp", None, None)
    return jax.shard_map(
        on_device,
        mesh=mesh,
        in_specs=(
            states, rows, pairs, rows, pairs, rows, rows, P("rep"),
            states, rows, pairs, rows, pairs, rows, rows,
            P(), P(None, "tp"), P(None, None, "tp"), P("tp"), P("tp"), P("tp"), P("tp"),
            P("tp", None),
        ),
        out_specs=(rows, rows, states),
        check_vma=False,
    )
```

```python
import functools

import jax
import jax.numpy as jnp
from jax import lax
from jax.experimental import pallas as pl
from jax.experimental.pallas import tpu as pltpu
from jax.sharding import PartitionSpec as P

F32 = jnp.float32
BF16 = jnp.bfloat16
ROWS = 64
INNER = 1024
STATE = 128
HEADS = 16
PAIRS = HEADS // 2
TAPS = 4
CAP = 3
NX, NZ = 4, 8
NY = 4
TOP = 8
PACK = 1056
EARLY = (0, 1, 7, 2, 6)
LATE = (3, 5, 4)
ORDER = EARLY + LATE
FIRST = ((1, 0), (3, 0))
SECOND = ((1, 1), (3, 1), (2, 0), (2, 1))
SPARE = ((1, 2), (3, 2), (1, 3), (3, 3), (2, 2))
SENDS = FIRST + SECOND + SPARE
VMEM_LIMIT = 58 * 1024 * 1024


def lanes_of(shape):
    return lax.broadcasted_iota(jnp.int32, shape, 1)


def rows_of(shape):
    return lax.broadcasted_iota(jnp.int32, shape, 0)


def mix_rows(win_x, win_bc, dt_pad, gated, dt, z_ref, params, load_state, store_state, normed, slot):
    wx, wbc, dt_bias, a_log, d_skip, norm_w = params
    coeffs = []
    for part in range(2):
        cols = slice(part * STATE, part * STATE + STATE)
        acc = win_bc[TOP - 3 : TOP - 3 + ROWS, cols] * wbc[0, part : part + 1, :]
        for k in range(1, TAPS):
            acc += win_bc[TOP - 3 + k : TOP - 3 + k + ROWS, cols] * wbc[k, part : part + 1, :]
        coeffs.append((acc / (1.0 + jnp.exp(-acc))).astype(BF16))
    coeff_b, coeff_c = coeffs

    dt_pad[...] = jnp.zeros_like(dt_pad)
    dt_pad[0:HEADS, 0:ROWS] = dt[0].astype(F32)
    raw = dt_pad[...].T[0:ROWS, 0:HEADS] + dt_bias[...]
    step = jnp.maximum(raw, 0.0) + jnp.log(1.0 + jnp.exp(-jnp.abs(raw)))
    dt_pad[...] = jnp.zeros_like(dt_pad)
    dt_pad[0:ROWS, 0:HEADS] = step
    dt_pad[ROWS:, 0:HEADS] = step * -jnp.exp(a_log[...])
    size = dt_pad[0:ROWS]
    cum = dt_pad[ROWS:]
    row = rows_of((ROWS, 128))
    for shift in (1, 2, 4, 8, 16, 32):
        cum = cum + jnp.where(row >= shift, pltpu.roll(cum, shift, 0), 0.0)

    lane = lanes_of((ROWS, 128))
    left = lane < 64
    source = jnp.where(left, lane, lane - 64)
    causal = row >= source
    diagonal = row == source
    twice_b = jnp.concatenate([coeff_b, coeff_b], axis=0)
    scores = lax.dot_general(
        coeff_c, twice_b, (((1,), (1,)), ((), ())), preferred_element_type=F32
    )
    squares = jnp.zeros((ROWS, 128), F32)
    for pair in range(PAIRS):
        cols = slice(pair * 128, pair * 128 + 128)
        first, second = 2 * pair, 2 * pair + 1

        def spread(values):
            return jnp.where(left, values[:, first : first + 1], values[:, second : second + 1])

        acc = win_x[TOP - 3 : TOP - 3 + ROWS, cols] * wx[0:1, cols]
        for k in range(1, TAPS):
            acc += win_x[TOP - 3 + k : TOP - 3 + k + ROWS, cols] * wx[k : k + 1, cols]
        x_conv = acc / (1.0 + jnp.exp(-acc))
        cum_here = spread(cum)
        x_size = x_conv * spread(size)
        cum_source = jnp.sum(jnp.where(diagonal, cum_here, 0.0), axis=0, keepdims=True)
        decay = jnp.where(causal, jnp.exp(jnp.where(causal, cum_here - cum_source, 0.0)), 0.0)
        weights = (decay * scores).astype(BF16)
        blocks = jnp.concatenate(
            [jnp.where(left, x_size, 0.0), jnp.where(left, 0.0, x_size)], axis=0
        ).astype(BF16)
        y = jnp.dot(weights, blocks, preferred_element_type=F32)
        held = load_state(pair)
        y += jnp.exp(cum_here) * lax.dot_general(
            coeff_c, held, (((1,), (1,)), ((), ())), preferred_element_type=F32
        )
        y += spread(d_skip[...]) * x_conv
        if store_state is not None:
            last = cum_here[ROWS - 1 : ROWS, :]
            tail = (jnp.exp(last - cum_here) * x_size).astype(BF16)
            update = lax.dot_general(
                tail, coeff_b, (((0,), (0,)), ((), ())), preferred_element_type=F32
            )
            final = jnp.exp(cum[ROWS - 1 : ROWS, :])
            keep = jnp.where(
                rows_of((128, 128)) < 64, final[:, first : first + 1], final[:, second : second + 1]
            )
            store_state(pair, held.astype(F32) * keep + update)
        gate = z_ref[0, :, cols].astype(F32)
        g = y * (gate / (1.0 + jnp.exp(-gate)))
        gated[:, cols] = g
        squares += g * g
    scale = lax.rsqrt(jnp.sum(squares, axis=1, keepdims=True) * (1.0 / INNER) + 1e-05)
    normed[pl.ds(slot * ROWS, ROWS), :] = (gated[...] * scale * norm_w[...]).astype(BF16)


def load_pairs(win_bc, bc):
    both = bc[0].astype(F32)
    win_bc[TOP:, :STATE] = both[:, 0, :]
    win_bc[TOP:, STATE:] = both[:, 1, :]


def project(blocks, normed, weight, sent, kept):
    width = sent.shape[2]
    for at, out in ((0, sent), (NY, kept)):
        for k in range(NY):
            start = pl.multiple_of(blocks[at + k] * width, width)
            out[k] = jnp.dot(
                normed[...], weight[:, pl.ds(start, width)], preferred_element_type=F32
            ).astype(BF16)


def resident_kernel(
    count, blocks, out_w, state, conv_x, conv_bc, x, bc, z, dt,
    wx, wbc, dt_bias, a_log, d_skip, norm_w, sent, kept, conv_rows, normed, weight,
    weight_sem, win_x, win_bc, dt_pad, gated,
):
    slot = pl.program_id(0)
    fetch = pltpu.make_async_copy(out_w, weight, weight_sem)

    @pl.when(slot == 0)
    def _():
        fetch.start()
        conv_rows[...] = conv_x[...].astype(F32)

    @pl.when(slot < count[0])
    def _():
        for k in range(TAPS - 1):
            win_x[TOP - 3 + k : TOP - 2 + k, :] = conv_rows[k, pl.ds(slot, 1), :]
        win_x[TOP:, :] = x[0].astype(F32)
        for k in range(TAPS - 1):
            both = conv_bc[0, k].astype(F32)
            for part in range(2):
                win_bc[TOP - 3 + k : TOP - 2 + k, part * STATE : part * STATE + STATE] = both[
                    part : part + 1
                ]
        load_pairs(win_bc, bc)

        def load_state(pair):
            return state[0, 2 * pair : 2 * pair + 2].reshape(128, STATE)

        mix_rows(
            win_x, win_bc, dt_pad, gated, dt, z,
            (wx, wbc, dt_bias, a_log, d_skip, norm_w), load_state, None, normed, slot,
        )

    @pl.when(slot >= count[0])
    def _():
        normed[pl.ds(slot * ROWS, ROWS), :] = jnp.zeros((ROWS, INNER), BF16)

    @pl.when(slot == pl.num_programs(0) - 1)
    def _():
        fetch.wait()
        project(blocks, normed, weight, sent, kept)


ROW_SCRATCH = [
    pltpu.VMEM((TOP + ROWS, INNER), F32),
    pltpu.VMEM((TOP + ROWS, 2 * STATE), F32),
    pltpu.VMEM((2 * ROWS, 128), F32),
    pltpu.VMEM((ROWS, INNER), F32),
]


def whole(array):
    return pl.BlockSpec(array.shape, lambda *_: (0,) * array.ndim)


def per_slot(shape):
    return pl.BlockSpec((1,) + shape, lambda i, *_: (i,) + (0,) * len(shape))


def row_scratch(slots):
    return [
        pltpu.VMEM((slots * ROWS, INNER), BF16),
        pltpu.VMEM((INNER, 4096), BF16),
        pltpu.SemaphoreType.DMA,
    ] + ROW_SCRATCH


def partial_sums(slots):
    shape = (NY, slots * ROWS, 4096 // 8)
    return [jax.ShapeDtypeStruct(shape, BF16)] * 2


def resident_rows(count, blocks, out_w, state, conv_x, conv_bc, x, bc, z, dt, params):
    slots = state.shape[0]
    sums = partial_sums(slots)
    return pl.pallas_call(
        resident_kernel,
        grid=(slots,),
        in_specs=[pl.BlockSpec(memory_space=pltpu.SMEM)] * 2
        + [pl.BlockSpec(memory_space=pl.ANY), per_slot(state.shape[1:]), whole(conv_x)]
        + [per_slot(a.shape[1:]) for a in (conv_bc, x, bc, z, dt)]
        + [whole(a) for a in params],
        out_specs=[whole(a) for a in sums],
        out_shape=sums,
        scratch_shapes=[pltpu.VMEM((TAPS - 1, slots, INNER), F32)] + row_scratch(slots),
        compiler_params=pltpu.CompilerParams(vmem_limit_bytes=VMEM_LIMIT),
        cost_estimate=pl.CostEstimate(
            flops=3_000_000_000, bytes_accessed=16_000_000, transcendentals=0
        ),
        name="resident_rows",
    )(count, blocks, out_w, state, conv_x, conv_bc, x, bc, z, dt, *params)


def line_hits(assign, target, column):
    target_z = lax.rem(target, NZ)
    return [
        (assign[column * NZ + lax.rem(target_z + NZ - offset, NZ)] == target).astype(jnp.int32)
        for offset in ORDER
    ]


def send_ranks(hits, shift):
    seen = jnp.int32(0)
    if shift != 2:
        seen = 1 - functools.reduce(jnp.maximum, hits[: len(EARLY)])
    ranks = []
    for hit in hits:
        ranks.append(seen)
        seen = seen + hit
    return ranks


def forward_kernel(sends, offsets, info, *refs):
    packets = dict(zip(offsets, refs))
    outs, sems = refs[len(offsets) : -1], refs[-1]
    me = info[32]
    column, z = lax.div(me, NZ), lax.rem(me, NZ)
    todo = []
    for slot, (shift, wanted) in enumerate(sends):
        target = lax.rem(column + shift, NX) * NZ + z
        hits = line_hits(info, target, column)
        for offset, hit, rank in zip(ORDER, hits, send_ranks(hits, shift)):
            if offset in packets:
                todo.append(
                    ((hit == 1) & (rank == wanted),
                     pltpu.make_async_copy(packets[offset], outs[slot], sems.at[slot]))
                )
    if 4 not in offsets:
        slot = len(sends)
        even = lax.rem(z, 2) == 0
        for when, offset in ((even, 2), (jnp.logical_not(even), 6)):
            todo.append(
                (when, pltpu.make_async_copy(packets[offset], outs[slot], sems.at[slot]))
            )
    for wanted, copy in todo:
        pl.when(wanted)(copy.start)
    for wanted, copy in todo:
        pl.when(wanted)(copy.wait)


def forward(sends, offsets, info, packets):
    count = len(sends) + (0 if 4 in offsets else 1)
    return pl.pallas_call(
        functools.partial(forward_kernel, sends, offsets),
        in_specs=[pl.BlockSpec(memory_space=pltpu.SMEM)]
        + [pl.BlockSpec(memory_space=pl.ANY)] * len(packets),
        out_specs=[pl.BlockSpec(memory_space=pl.ANY)] * count,
        out_shape=[jax.ShapeDtypeStruct((PACK, 128), BF16)] * count,
        scratch_shapes=[pltpu.SemaphoreType.DMA((count,))],
        cost_estimate=pl.CostEstimate(flops=0, bytes_accessed=3_000_000, transcendentals=0),
        name="forward",
    )(info, *packets)


def blank_kernel(info, *outs):
    pass


def blank(info, count):
    return pl.pallas_call(
        blank_kernel,
        in_specs=[pl.BlockSpec(memory_space=pltpu.SMEM)],
        out_specs=[pl.BlockSpec(memory_space=pl.ANY)] * count,
        out_shape=[jax.ShapeDtypeStruct((PACK, 128), BF16)] * count,
        name="blank",
    )(info)


PACKETS = len(ORDER)
ARRIVED = len(SENDS)


def slot_kernel(info, blocks, out_w, *refs):
    line, rest = refs[:PACKETS], refs[PACKETS:]
    came, rest = rest[:ARRIVED], rest[ARRIVED:]
    (x, bc, z, dt, wx, wbc, dt_bias, a_log, d_skip, norm_w, sent, kept, state,
     held, valid, sems, normed, weight, weight_sem, win_x, win_bc, dt_pad, gated) = rest
    fetch = pltpu.make_async_copy(out_w, weight, weight_sem)
    packets = dict(zip(ORDER, line))
    arrived = dict(zip(SENDS, came))
    slot = pl.program_id(0)
    me = info[32]
    column, my_z = lax.div(me, NZ), lax.rem(me, NZ)

    @pl.when(slot == 0)
    def _():
        before = jnp.int32(0)
        for request in range(NX * NZ):
            valid[request] = before
            before = before + (info[request] == me).astype(jnp.int32)
        valid[NX * NZ] = before
        for shift in range(NX):
            sender = lax.rem(column + NX - shift, NX)
            hits = line_hits(info, me, sender)
            for offset, hit, rank in zip(ORDER, hits, send_ranks(hits, shift)):
                source = sender * NZ + lax.rem(my_z + NZ - offset, NZ)
                place = valid[source]

                @pl.when(hit == 1)
                def _(shift=shift, offset=offset, rank=rank, place=place):
                    if shift == 0:
                        pltpu.make_async_copy(
                            packets[offset], held.at[place], sems.at[place]
                        ).start()
                    for (over, n), packet in arrived.items():
                        if over == shift:
                            @pl.when(rank == n)
                            def _(packet=packet):
                                pltpu.make_async_copy(
                                    packet, held.at[place], sems.at[place]
                                ).start()
        fetch.start()

    live = slot < valid[NX * NZ]

    @pl.when(live)
    def _():
        win_x[TOP:, :] = x[0].astype(F32)
        load_pairs(win_bc, bc)
        pltpu.make_async_copy(held.at[slot], held.at[slot], sems.at[slot]).wait()
        conv = held[slot, 1024:PACK, :].astype(F32)
        for k in range(TAPS - 1):
            for b in range(8):
                win_x[TOP - 3 + k : TOP - 2 + k, 128 * b : 128 * b + 128] = conv[
                    8 * k + b : 8 * k + b + 1
                ]
            for b in range(2):
                win_bc[TOP - 3 + k : TOP - 2 + k, 128 * b : 128 * b + 128] = conv[
                    24 + 2 * k + b : 25 + 2 * k + b
                ]

        def load_state(pair):
            return held[slot, 128 * pair : 128 * pair + 128, :]

        def store_state(pair, value):
            state[0, 2 * pair : 2 * pair + 2] = value.astype(BF16).reshape(2, 64, STATE)

        mix_rows(
            win_x, win_bc, dt_pad, gated, dt, z,
            (wx, wbc, dt_bias, a_log, d_skip, norm_w), load_state, store_state, normed, slot,
        )

    @pl.when(jnp.logical_not(live))
    def _():
        normed[pl.ds(slot * ROWS, ROWS), :] = jnp.zeros((ROWS, INNER), BF16)
        state[...] = jnp.zeros_like(state)

    @pl.when(slot == pl.num_programs(0) - 1)
    def _():
        fetch.wait()
        project(blocks, normed, weight, sent, kept)


def slot_rows(info, blocks, out_w, line, came, x, bc, z, dt, params):
    slots = x.shape[0]
    sums = partial_sums(slots)
    return pl.pallas_call(
        slot_kernel,
        grid=(slots,),
        in_specs=[pl.BlockSpec(memory_space=pltpu.SMEM)] * 2
        + [pl.BlockSpec(memory_space=pl.ANY)] * (1 + PACKETS + ARRIVED)
        + [per_slot(a.shape[1:]) for a in (x, bc, z, dt)]
        + [whole(a) for a in params],
        out_specs=[whole(a) for a in sums] + [per_slot((HEADS, 64, STATE))],
        out_shape=sums + [jax.ShapeDtypeStruct((slots, HEADS, 64, STATE), BF16)],
        scratch_shapes=[
            pltpu.VMEM((CAP, PACK, 128), BF16),
            pltpu.SMEM((NX * NZ + 1,), jnp.int32),
            pltpu.SemaphoreType.DMA((CAP,)),
        ]
        + row_scratch(slots),
        compiler_params=pltpu.CompilerParams(vmem_limit_bytes=VMEM_LIMIT),
        cost_estimate=pl.CostEstimate(
            flops=3_000_000_000, bytes_accessed=20_000_000, transcendentals=0
        ),
        name="slot_rows",
    )(info, blocks, out_w, *line, *came, x, bc, z, dt, *params)


def across_cores(array):
    return lax.ppermute(array, "tp", [(t, t ^ 1) for t in range(2 * NY)])


def chip_sums(own, from_mate):
    return [own[k].astype(F32) + from_mate[k].astype(F32) for k in range(NY)]


def reduce_out(chip, slots):
    total = chip[0]
    for k in range(1, NY):
        shifted = [(t, (t + 2 * k) % (2 * NY)) for t in range(2 * NY)]
        total = total + lax.ppermute(chip[k].astype(BF16), "tp", shifted).astype(F32)
    return total.astype(BF16).reshape(slots, ROWS, -1)


def along_z(array, step):
    pairs = [(x * NZ + z, x * NZ + (z + step) % NZ) for x in range(NX) for z in range(NZ)]
    return lax.ppermute(array, "rep", pairs)


def across_z(array):
    pairs = [
        (x * NZ + z, x * NZ + (z + (2 if z % 2 == 0 else -2)) % NZ)
        for x in range(NX) for z in range(NZ)
    ]
    return lax.ppermute(array, "rep", pairs)


def along_x(sends, arrays):
    return [
        lax.ppermute(
            array, "rep",
            [(x * NZ + z, (x + shift) % NX * NZ + z) for x in range(NX) for z in range(NZ)],
        )
        for (shift, _), array in zip(sends, arrays)
    ]


def on_device(
    res_state, res_conv_x, res_conv_bc, res_x, res_bc, res_z, res_dt, res_count,
    hand_state, hand_conv_x, hand_conv_bc, slot_x, slot_bc, slot_z, slot_dt,
    assignment, conv_wx, conv_wbc, dt_bias, a_log, d_skip, norm_w, out_w,
):
    me = lax.axis_index("rep")
    tp = lax.axis_index("tp")
    info = jnp.concatenate([assignment, me[None].astype(jnp.int32)])
    packet = jnp.concatenate(
        [
            hand_state.reshape(-1, STATE),
            hand_conv_x.reshape(-1, STATE),
            hand_conv_bc.reshape(-1, STATE),
            jnp.zeros((2, STATE), BF16),
        ],
        axis=0,
    )
    up1, down1 = along_z(packet, 1), along_z(packet, -1)
    up2, down2 = along_z(packet, 2), along_z(packet, -2)

    params = (
        conv_wx, conv_wbc, dt_bias[None], a_log[None], d_skip[None],
        norm_w[None],
    )
    chip, core = tp // 2, tp % 2
    turns = (chip + jnp.arange(NY, dtype=jnp.int32)) % NY
    chips = jnp.arange(NY, dtype=jnp.int32)
    blocks = jnp.concatenate([2 * turns + 1 - core, 2 * turns + core])
    res_blocks = jnp.concatenate([2 * chips + 1 - core, 2 * chips + core])
    res_sent, res_kept = resident_rows(
        res_count, res_blocks, out_w, res_state, res_conv_x.transpose(1, 0, 2),
        res_conv_bc, res_x, res_bc, res_z, res_dt.transpose(0, 2, 1), params,
    )
    res_chip = (res_kept.astype(F32) + across_cores(res_sent).astype(F32)).astype(BF16)
    up1, down1, up2, down2, res_chip = lax.optimization_barrier(
        (up1, down1, up2, down2, res_chip)
    )

    early = [packet, up1, down1, up2, down2]
    *ahead, far = forward(FIRST, EARLY, info, early)
    far = across_z(far)
    up3, down3 = along_z(up2, 1), along_z(down2, -1)
    first = along_x(FIRST, ahead)
    up3, down3, far, *first = lax.optimization_barrier((up3, down3, far, *first))
    line = early + [up3, down3, far]
    ahead = forward(SECOND, ORDER, info, line)
    *ahead, info, res_chip = lax.optimization_barrier((*ahead, info, res_chip))
    second = along_x(SECOND, ahead)
    res_parts = lax.all_to_all(
        res_chip, "tp", 0, 0, axis_index_groups=[[0, 2, 4, 6], [1, 3, 5, 7]], tiled=True
    )

    ids = jnp.arange(NX * NZ)
    goes = assignment[None, :] == ids[:, None]
    offset = (ids[:, None] - ids[None, :]) % NZ
    far = (offset > 2) & (offset < 6)
    all_hits = jnp.sum(goes.reshape(-1, NX, NZ), axis=2)
    near_hits = jnp.sum((goes & ~far).reshape(-1, NX, NZ), axis=2)
    shift = (ids[:, None] // NZ - jnp.arange(NX)[None, :]) % NX
    room = jnp.where(shift == 2, 2, jnp.where(shift == 0, NZ, 1 + jnp.minimum(near_hits, 1)))
    more = jnp.any(all_hits > room)
    third = lax.cond(
        more,
        lambda *held: tuple(along_x(SPARE, forward(SPARE, ORDER, held[0], held[1:]))),
        lambda *held: tuple(blank(held[0], len(SPARE))),
        info, *line,
    )
    res_out = jnp.sum(res_parts.astype(F32), axis=0).astype(BF16)
    res_out = res_out.reshape(res_state.shape[0], ROWS, -1)
    *second, res_out = lax.optimization_barrier((*second, res_out))
    sent, kept, slot_state = slot_rows(
        info, blocks, out_w, line, first + second + list(third), slot_x, slot_bc, slot_z,
        slot_dt.transpose(0, 2, 1), params,
    )
    slot_out = reduce_out(chip_sums(kept, across_cores(sent)), slot_x.shape[0])
    return res_out, slot_out, slot_state


def solution(mesh):
    rows = P("rep", None, "tp")
    pairs = P("rep", None, None, "tp")
    states = P("rep", "tp", None, None)
    return jax.shard_map(
        on_device,
        mesh=mesh,
        in_specs=(
            states, rows, pairs, rows, pairs, rows, rows, P("rep"),
            states, rows, pairs, rows, pairs, rows, rows,
            P(), P(None, "tp"), P(None, None, "tp"), P("tp"), P("tp"), P("tp"), P("tp"),
            P("tp", None),
        ),
        out_specs=(rows, rows, states),
        check_vma=False,
    )
```

```python
import functools

import jax
import jax.numpy as jnp
from jax import lax
from jax.experimental import pallas as pl
from jax.experimental.pallas import tpu as pltpu
from jax.sharding import PartitionSpec as P

F32 = jnp.float32
BF16 = jnp.bfloat16
ROWS = 64
INNER = 1024
STATE = 128
HEADS = 16
PAIRS = HEADS // 2
TAPS = 4
CAP = 3
NX, NZ = 4, 8
NY = 4
TOP = 8
PACK = 1056
EARLY = (0, 1, 7, 2, 6)
LATE = (3, 5, 4)
ORDER = EARLY + LATE
FIRST = ((1, 0), (3, 0))
SECOND = ((1, 1), (3, 1), (2, 0), (2, 1))
SPARE = ((1, 2), (3, 2), (1, 3), (3, 3), (2, 2))
SENDS = FIRST + SECOND + SPARE
VMEM_LIMIT = 58 * 1024 * 1024


def lanes_of(shape):
    return lax.broadcasted_iota(jnp.int32, shape, 1)


def rows_of(shape):
    return lax.broadcasted_iota(jnp.int32, shape, 0)


def mix_rows(win_x, win_bc, dt_pad, gated, dt, z_ref, params, load_state, store_state, normed, slot):
    wx, wbc, dt_bias, a_log, d_skip, norm_w = params
    coeffs = []
    for part in range(2):
        cols = slice(part * STATE, part * STATE + STATE)
        acc = win_bc[TOP - 3 : TOP - 3 + ROWS, cols] * wbc[0, part : part + 1, :]
        for k in range(1, TAPS):
            acc += win_bc[TOP - 3 + k : TOP - 3 + k + ROWS, cols] * wbc[k, part : part + 1, :]
        coeffs.append((acc / (1.0 + jnp.exp(-acc))).astype(BF16))
    coeff_b, coeff_c = coeffs

    dt_pad[...] = jnp.zeros_like(dt_pad)
    dt_pad[0:HEADS, 0:ROWS] = dt[0].astype(F32)
    raw = dt_pad[...].T[0:ROWS, 0:HEADS] + dt_bias[...]
    step = jnp.maximum(raw, 0.0) + jnp.log(1.0 + jnp.exp(-jnp.abs(raw)))
    dt_pad[...] = jnp.zeros_like(dt_pad)
    dt_pad[0:ROWS, 0:HEADS] = step
    dt_pad[ROWS:, 0:HEADS] = step * -jnp.exp(a_log[...])
    size = dt_pad[0:ROWS]
    cum = dt_pad[ROWS:]
    row = rows_of((ROWS, 128))
    for shift in (1, 2, 4, 8, 16, 32):
        cum = cum + jnp.where(row >= shift, pltpu.roll(cum, shift, 0), 0.0)

    lane = lanes_of((ROWS, 128))
    left = lane < 64
    source = jnp.where(left, lane, lane - 64)
    causal = row >= source
    diagonal = row == source
    twice_b = jnp.concatenate([coeff_b, coeff_b], axis=0)
    scores = lax.dot_general(
        coeff_c, twice_b, (((1,), (1,)), ((), ())), preferred_element_type=F32
    )
    squares = jnp.zeros((ROWS, 128), F32)
    for pair in range(PAIRS):
        cols = slice(pair * 128, pair * 128 + 128)
        first, second = 2 * pair, 2 * pair + 1

        def spread(values):
            return jnp.where(left, values[:, first : first + 1], values[:, second : second + 1])

        acc = win_x[TOP - 3 : TOP - 3 + ROWS, cols] * wx[0:1, cols]
        for k in range(1, TAPS):
            acc += win_x[TOP - 3 + k : TOP - 3 + k + ROWS, cols] * wx[k : k + 1, cols]
        x_conv = acc / (1.0 + jnp.exp(-acc))
        cum_here = spread(cum)
        x_size = x_conv * spread(size)
        cum_source = jnp.sum(jnp.where(diagonal, cum_here, 0.0), axis=0, keepdims=True)
        decay = jnp.where(causal, jnp.exp(jnp.where(causal, cum_here - cum_source, 0.0)), 0.0)
        weights = (decay * scores).astype(BF16)
        blocks = jnp.concatenate(
            [jnp.where(left, x_size, 0.0), jnp.where(left, 0.0, x_size)], axis=0
        ).astype(BF16)
        y = jnp.dot(weights, blocks, preferred_element_type=F32)
        held = load_state(pair)
        y += jnp.exp(cum_here) * lax.dot_general(
            coeff_c, held, (((1,), (1,)), ((), ())), preferred_element_type=F32
        )
        y += spread(d_skip[...]) * x_conv
        if store_state is not None:
            last = cum_here[ROWS - 1 : ROWS, :]
            tail = (jnp.exp(last - cum_here) * x_size).astype(BF16)
            update = lax.dot_general(
                tail, coeff_b, (((0,), (0,)), ((), ())), preferred_element_type=F32
            )
            final = jnp.exp(cum[ROWS - 1 : ROWS, :])
            keep = jnp.where(
                rows_of((128, 128)) < 64, final[:, first : first + 1], final[:, second : second + 1]
            )
            store_state(pair, held.astype(F32) * keep + update)
        gate = z_ref[0, :, cols].astype(F32)
        g = y * (gate / (1.0 + jnp.exp(-gate)))
        gated[:, cols] = g
        squares += g * g
    scale = lax.rsqrt(jnp.sum(squares, axis=1, keepdims=True) * (1.0 / INNER) + 1e-05)
    normed[pl.ds(slot * ROWS, ROWS), :] = (gated[...] * scale * norm_w[...]).astype(BF16)


def load_pairs(win_bc, bc):
    both = bc[0].astype(F32)
    win_bc[TOP:, :STATE] = both[:, 0, :]
    win_bc[TOP:, STATE:] = both[:, 1, :]


def project(blocks, normed, weight, sent, kept):
    width = sent.shape[2]
    for at, out in ((0, sent), (NY, kept)):
        for k in range(NY):
            start = pl.multiple_of(blocks[at + k] * width, width)
            out[k] = jnp.dot(
                normed[...], weight[:, pl.ds(start, width)], preferred_element_type=F32
            ).astype(BF16)


def resident_kernel(
    count, blocks, out_w, state, conv_x, conv_bc, x, bc, z, dt,
    wx, wbc, dt_bias, a_log, d_skip, norm_w, parts, conv_rows, normed, weight,
    weight_sem, win_x, win_bc, dt_pad, gated,
):
    slot = pl.program_id(0)
    fetch = pltpu.make_async_copy(out_w, weight, weight_sem)

    @pl.when(slot == 0)
    def _():
        fetch.start()
        conv_rows[...] = conv_x[...].astype(F32)

    @pl.when(slot < count[0])
    def _():
        for k in range(TAPS - 1):
            win_x[TOP - 3 + k : TOP - 2 + k, :] = conv_rows[k, pl.ds(slot, 1), :]
        win_x[TOP:, :] = x[0].astype(F32)
        for k in range(TAPS - 1):
            both = conv_bc[0, k].astype(F32)
            for part in range(2):
                win_bc[TOP - 3 + k : TOP - 2 + k, part * STATE : part * STATE + STATE] = both[
                    part : part + 1
                ]
        load_pairs(win_bc, bc)

        def load_state(pair):
            return state[0, 2 * pair : 2 * pair + 2].reshape(128, STATE)

        mix_rows(
            win_x, win_bc, dt_pad, gated, dt, z,
            (wx, wbc, dt_bias, a_log, d_skip, norm_w), load_state, None, normed, slot,
        )

    @pl.when(slot >= count[0])
    def _():
        normed[pl.ds(slot * ROWS, ROWS), :] = jnp.zeros((ROWS, INNER), BF16)

    @pl.when(slot == pl.num_programs(0) - 1)
    def _():
        fetch.wait()
        project(blocks, normed, weight, parts.at[0:NY], parts.at[NY:])


ROW_SCRATCH = [
    pltpu.VMEM((TOP + ROWS, INNER), F32),
    pltpu.VMEM((TOP + ROWS, 2 * STATE), F32),
    pltpu.VMEM((2 * ROWS, 128), F32),
    pltpu.VMEM((ROWS, INNER), F32),
]


def whole(array):
    return pl.BlockSpec(array.shape, lambda *_: (0,) * array.ndim)


def per_slot(shape):
    return pl.BlockSpec((1,) + shape, lambda i, *_: (i,) + (0,) * len(shape))


def row_scratch(slots):
    return [
        pltpu.VMEM((slots * ROWS, INNER), BF16),
        pltpu.VMEM((INNER, 4096), BF16),
        pltpu.SemaphoreType.DMA,
    ] + ROW_SCRATCH


def partial_sums(slots):
    shape = (NY, slots * ROWS, 4096 // 8)
    return [jax.ShapeDtypeStruct(shape, BF16)] * 2


def resident_rows(count, blocks, out_w, state, conv_x, conv_bc, x, bc, z, dt, params):
    slots = state.shape[0]
    parts = jax.ShapeDtypeStruct((2 * NY, slots * ROWS, out_w.shape[1] // 8), BF16)
    return pl.pallas_call(
        resident_kernel,
        grid=(slots,),
        in_specs=[pl.BlockSpec(memory_space=pltpu.SMEM)] * 2
        + [pl.BlockSpec(memory_space=pl.ANY), per_slot(state.shape[1:]), whole(conv_x)]
        + [per_slot(a.shape[1:]) for a in (conv_bc, x, bc, z, dt)]
        + [whole(a) for a in params],
        out_specs=whole(parts),
        out_shape=parts,
        scratch_shapes=[pltpu.VMEM((TAPS - 1, slots, INNER), F32)] + row_scratch(slots),
        compiler_params=pltpu.CompilerParams(vmem_limit_bytes=VMEM_LIMIT),
        cost_estimate=pl.CostEstimate(
            flops=3_000_000_000, bytes_accessed=16_000_000, transcendentals=0
        ),
        name="resident_rows",
    )(count, blocks, out_w, state, conv_x, conv_bc, x, bc, z, dt, *params)


def line_hits(assign, target, column):
    target_z = lax.rem(target, NZ)
    return [
        (assign[column * NZ + lax.rem(target_z + NZ - offset, NZ)] == target).astype(jnp.int32)
        for offset in ORDER
    ]


def send_ranks(hits, shift):
    seen = jnp.int32(0)
    if shift != 2:
        seen = 1 - functools.reduce(jnp.maximum, hits[: len(EARLY)])
    ranks = []
    for hit in hits:
        ranks.append(seen)
        seen = seen + hit
    return ranks


def forward_kernel(sends, offsets, info, *refs):
    packets = dict(zip(offsets, refs))
    outs, sems = refs[len(offsets) : -1], refs[-1]
    me = info[32]
    column, z = lax.div(me, NZ), lax.rem(me, NZ)
    todo = []
    for slot, (shift, wanted) in enumerate(sends):
        target = lax.rem(column + shift, NX) * NZ + z
        hits = line_hits(info, target, column)
        for offset, hit, rank in zip(ORDER, hits, send_ranks(hits, shift)):
            if offset in packets:
                todo.append(
                    ((hit == 1) & (rank == wanted),
                     pltpu.make_async_copy(packets[offset], outs[slot], sems.at[slot]))
                )
    if 4 not in offsets:
        slot = len(sends)
        even = lax.rem(z, 2) == 0
        for when, offset in ((even, 2), (jnp.logical_not(even), 6)):
            todo.append(
                (when, pltpu.make_async_copy(packets[offset], outs[slot], sems.at[slot]))
            )
    for wanted, copy in todo:
        pl.when(wanted)(copy.start)
    for wanted, copy in todo:
        pl.when(wanted)(copy.wait)


def forward(sends, offsets, info, packets):
    count = len(sends) + (0 if 4 in offsets else 1)
    return pl.pallas_call(
        functools.partial(forward_kernel, sends, offsets),
        in_specs=[pl.BlockSpec(memory_space=pltpu.SMEM)]
        + [pl.BlockSpec(memory_space=pl.ANY)] * len(packets),
        out_specs=[pl.BlockSpec(memory_space=pl.ANY)] * count,
        out_shape=[jax.ShapeDtypeStruct((PACK, 128), BF16)] * count,
        scratch_shapes=[pltpu.SemaphoreType.DMA((count,))],
        cost_estimate=pl.CostEstimate(flops=0, bytes_accessed=3_000_000, transcendentals=0),
        name="forward",
    )(info, *packets)


def blank_kernel(info, *outs):
    pass


def blank(info, count):
    return pl.pallas_call(
        blank_kernel,
        in_specs=[pl.BlockSpec(memory_space=pltpu.SMEM)],
        out_specs=[pl.BlockSpec(memory_space=pl.ANY)] * count,
        out_shape=[jax.ShapeDtypeStruct((PACK, 128), BF16)] * count,
        name="blank",
    )(info)


PACKETS = len(ORDER)
ARRIVED = len(SENDS)


def slot_kernel(info, blocks, out_w, *refs):
    line, rest = refs[:PACKETS], refs[PACKETS:]
    came, rest = rest[:ARRIVED], rest[ARRIVED:]
    (x, bc, z, dt, wx, wbc, dt_bias, a_log, d_skip, norm_w, sent, kept, state,
     held, valid, sems, normed, weight, weight_sem, win_x, win_bc, dt_pad, gated) = rest
    fetch = pltpu.make_async_copy(out_w, weight, weight_sem)
    packets = dict(zip(ORDER, line))
    arrived = dict(zip(SENDS, came))
    slot = pl.program_id(0)
    me = info[32]
    column, my_z = lax.div(me, NZ), lax.rem(me, NZ)

    @pl.when(slot == 0)
    def _():
        before = jnp.int32(0)
        for request in range(NX * NZ):
            valid[request] = before
            before = before + (info[request] == me).astype(jnp.int32)
        valid[NX * NZ] = before
        for shift in range(NX):
            sender = lax.rem(column + NX - shift, NX)
            hits = line_hits(info, me, sender)
            for offset, hit, rank in zip(ORDER, hits, send_ranks(hits, shift)):
                source = sender * NZ + lax.rem(my_z + NZ - offset, NZ)
                place = valid[source]

                @pl.when(hit == 1)
                def _(shift=shift, offset=offset, rank=rank, place=place):
                    if shift == 0:
                        pltpu.make_async_copy(
                            packets[offset], held.at[place], sems.at[place]
                        ).start()
                    for (over, n), packet in arrived.items():
                        if over == shift:
                            @pl.when(rank == n)
                            def _(packet=packet):
                                pltpu.make_async_copy(
                                    packet, held.at[place], sems.at[place]
                                ).start()
        fetch.start()

    live = slot < valid[NX * NZ]

    @pl.when(live)
    def _():
        win_x[TOP:, :] = x[0].astype(F32)
        load_pairs(win_bc, bc)
        pltpu.make_async_copy(held.at[slot], held.at[slot], sems.at[slot]).wait()
        conv = held[slot, 1024:PACK, :].astype(F32)
        for k in range(TAPS - 1):
            for b in range(8):
                win_x[TOP - 3 + k : TOP - 2 + k, 128 * b : 128 * b + 128] = conv[
                    8 * k + b : 8 * k + b + 1
                ]
            for b in range(2):
                win_bc[TOP - 3 + k : TOP - 2 + k, 128 * b : 128 * b + 128] = conv[
                    24 + 2 * k + b : 25 + 2 * k + b
                ]

        def load_state(pair):
            return held[slot, 128 * pair : 128 * pair + 128, :]

        def store_state(pair, value):
            state[0, 2 * pair : 2 * pair + 2] = value.astype(BF16).reshape(2, 64, STATE)

        mix_rows(
            win_x, win_bc, dt_pad, gated, dt, z,
            (wx, wbc, dt_bias, a_log, d_skip, norm_w), load_state, store_state, normed, slot,
        )

    @pl.when(jnp.logical_not(live))
    def _():
        normed[pl.ds(slot * ROWS, ROWS), :] = jnp.zeros((ROWS, INNER), BF16)
        state[...] = jnp.zeros_like(state)

    @pl.when(slot == pl.num_programs(0) - 1)
    def _():
        fetch.wait()
        project(blocks, normed, weight, sent, kept)


def slot_rows(info, blocks, out_w, line, came, x, bc, z, dt, params):
    slots = x.shape[0]
    sums = partial_sums(slots)
    return pl.pallas_call(
        slot_kernel,
        grid=(slots,),
        in_specs=[pl.BlockSpec(memory_space=pltpu.SMEM)] * 2
        + [pl.BlockSpec(memory_space=pl.ANY)] * (1 + PACKETS + ARRIVED)
        + [per_slot(a.shape[1:]) for a in (x, bc, z, dt)]
        + [whole(a) for a in params],
        out_specs=[whole(a) for a in sums] + [per_slot((HEADS, 64, STATE))],
        out_shape=sums + [jax.ShapeDtypeStruct((slots, HEADS, 64, STATE), BF16)],
        scratch_shapes=[
            pltpu.VMEM((CAP, PACK, 128), BF16),
            pltpu.SMEM((NX * NZ + 1,), jnp.int32),
            pltpu.SemaphoreType.DMA((CAP,)),
        ]
        + row_scratch(slots),
        compiler_params=pltpu.CompilerParams(vmem_limit_bytes=VMEM_LIMIT),
        cost_estimate=pl.CostEstimate(
            flops=3_000_000_000, bytes_accessed=20_000_000, transcendentals=0
        ),
        name="slot_rows",
    )(info, blocks, out_w, *line, *came, x, bc, z, dt, *params)


def across_cores(array):
    return lax.ppermute(array, "tp", [(t, t ^ 1) for t in range(2 * NY)])


def chip_sums(own, from_mate):
    return [own[k].astype(F32) + from_mate[k].astype(F32) for k in range(NY)]


def reduce_out(chip, slots):
    total = chip[0]
    for k in range(1, NY):
        shifted = [(t, (t + 2 * k) % (2 * NY)) for t in range(2 * NY)]
        total = total + lax.ppermute(chip[k].astype(BF16), "tp", shifted).astype(F32)
    return total.astype(BF16).reshape(slots, ROWS, -1)


def along_z(array, step):
    pairs = [(x * NZ + z, x * NZ + (z + step) % NZ) for x in range(NX) for z in range(NZ)]
    return lax.ppermute(array, "rep", pairs)


def across_z(array):
    pairs = [
        (x * NZ + z, x * NZ + (z + (2 if z % 2 == 0 else -2)) % NZ)
        for x in range(NX) for z in range(NZ)
    ]
    return lax.ppermute(array, "rep", pairs)


def along_x(sends, arrays):
    return [
        lax.ppermute(
            array, "rep",
            [(x * NZ + z, (x + shift) % NX * NZ + z) for x in range(NX) for z in range(NZ)],
        )
        for (shift, _), array in zip(sends, arrays)
    ]


def on_device(
    res_state, res_conv_x, res_conv_bc, res_x, res_bc, res_z, res_dt, res_count,
    hand_state, hand_conv_x, hand_conv_bc, slot_x, slot_bc, slot_z, slot_dt,
    assignment, conv_wx, conv_wbc, dt_bias, a_log, d_skip, norm_w, out_w,
):
    me = lax.axis_index("rep")
    tp = lax.axis_index("tp")
    info = jnp.concatenate([assignment, me[None].astype(jnp.int32)])
    packet = jnp.concatenate(
        [
            hand_state.reshape(-1, STATE),
            hand_conv_x.reshape(-1, STATE),
            hand_conv_bc.reshape(-1, STATE),
            jnp.zeros((2, STATE), BF16),
        ],
        axis=0,
    )
    up1, down1 = along_z(packet, 1), along_z(packet, -1)
    up2, down2 = along_z(packet, 2), along_z(packet, -2)

    params = (
        conv_wx, conv_wbc, dt_bias[None], a_log[None], d_skip[None],
        norm_w[None],
    )
    chip, core = tp // 2, tp % 2
    turns = (chip + jnp.arange(NY, dtype=jnp.int32)) % NY
    blocks = jnp.concatenate([2 * turns + 1 - core, 2 * turns + core])
    res_blocks = jnp.arange(2 * NY, dtype=jnp.int32)
    res_parts = resident_rows(
        res_count, res_blocks, out_w, res_state, res_conv_x.transpose(1, 0, 2),
        res_conv_bc, res_x, res_bc, res_z, res_dt.transpose(0, 2, 1), params,
    )
    up1, down1, up2, down2, res_parts = lax.optimization_barrier(
        (up1, down1, up2, down2, res_parts)
    )
    early = [packet, up1, down1, up2, down2]
    *ahead, far = forward(FIRST, EARLY, info, early)
    far = across_z(far)
    up3, down3 = along_z(up2, 1), along_z(down2, -1)
    first = along_x(FIRST, ahead)
    up3, down3, far, *first = lax.optimization_barrier((up3, down3, far, *first))
    line = early + [up3, down3, far]
    ahead = forward(SECOND, ORDER, info, line)
    *ahead, info, res_parts = lax.optimization_barrier((*ahead, info, res_parts))
    res_parts = lax.all_to_all(res_parts, "tp", 0, 0, tiled=True)
    second = along_x(SECOND, ahead)

    ids = jnp.arange(NX * NZ)
    goes = assignment[None, :] == ids[:, None]
    offset = (ids[:, None] - ids[None, :]) % NZ
    far = (offset > 2) & (offset < 6)
    all_hits = jnp.sum(goes.reshape(-1, NX, NZ), axis=2)
    near_hits = jnp.sum((goes & ~far).reshape(-1, NX, NZ), axis=2)
    shift = (ids[:, None] // NZ - jnp.arange(NX)[None, :]) % NX
    room = jnp.where(shift == 2, 2, jnp.where(shift == 0, NZ, 1 + jnp.minimum(near_hits, 1)))
    more = jnp.any(all_hits > room)
    third = lax.cond(
        more,
        lambda *held: tuple(along_x(SPARE, forward(SPARE, ORDER, held[0], held[1:]))),
        lambda *held: tuple(blank(held[0], len(SPARE))),
        info, *line,
    )
    res_out = jnp.sum(res_parts.astype(F32), axis=0).astype(BF16)
    res_out = res_out.reshape(res_state.shape[0], ROWS, -1)
    sent, kept, slot_state = slot_rows(
        info, blocks, out_w, line, first + second + list(third), slot_x, slot_bc, slot_z,
        slot_dt.transpose(0, 2, 1), params,
    )
    slot_out = reduce_out(chip_sums(kept, across_cores(sent)), slot_x.shape[0])
    return res_out, slot_out, slot_state


def solution(mesh):
    rows = P("rep", None, "tp")
    pairs = P("rep", None, None, "tp")
    states = P("rep", "tp", None, None)
    return jax.shard_map(
        on_device,
        mesh=mesh,
        in_specs=(
            states, rows, pairs, rows, pairs, rows, rows, P("rep"),
            states, rows, pairs, rows, pairs, rows, rows,
            P(), P(None, "tp"), P(None, None, "tp"), P("tp"), P("tp"), P("tp"), P("tp"),
            P("tp", None),
        ),
        out_specs=(rows, rows, states),
        check_vma=False,
    )
```

```python
import functools

import jax
import jax.numpy as jnp
from jax import lax
from jax.experimental import pallas as pl
from jax.experimental.pallas import tpu as pltpu
from jax.sharding import PartitionSpec as P

F32 = jnp.float32
BF16 = jnp.bfloat16
ROWS = 64
INNER = 1024
STATE = 128
HEADS = 16
PAIRS = HEADS // 2
TAPS = 4
CAP = 3
NX, NZ = 4, 8
NY = 4
TOP = 8
PACK = 1056
EARLY = (0, 1, 7, 2, 6)
LATE = (3, 5, 4)
ORDER = EARLY + LATE
FIRST = ((1, 0), (3, 0))
SECOND = ((1, 1), (3, 1), (2, 0), (2, 1))
SPARE = ((1, 2), (3, 2), (1, 3), (3, 3), (2, 2))
SENDS = FIRST + SECOND + SPARE
VMEM_LIMIT = 58 * 1024 * 1024


def lanes_of(shape):
    return lax.broadcasted_iota(jnp.int32, shape, 1)


def rows_of(shape):
    return lax.broadcasted_iota(jnp.int32, shape, 0)


def mix_rows(win_x, win_bc, dt_pad, gated, dt, z_ref, params, load_state, store_state, normed, slot):
    wx, wbc, dt_bias, a_log, d_skip, norm_w = params
    coeffs = []
    for part in range(2):
        cols = slice(part * STATE, part * STATE + STATE)
        acc = win_bc[TOP - 3 : TOP - 3 + ROWS, cols] * wbc[0, part : part + 1, :]
        for k in range(1, TAPS):
            acc += win_bc[TOP - 3 + k : TOP - 3 + k + ROWS, cols] * wbc[k, part : part + 1, :]
        coeffs.append((acc / (1.0 + jnp.exp(-acc))).astype(BF16))
    coeff_b, coeff_c = coeffs

    dt_pad[...] = jnp.zeros_like(dt_pad)
    dt_pad[0:HEADS, 0:ROWS] = dt[0].astype(F32)
    raw = dt_pad[...].T[0:ROWS, 0:HEADS] + dt_bias[...]
    step = jnp.maximum(raw, 0.0) + jnp.log(1.0 + jnp.exp(-jnp.abs(raw)))
    dt_pad[...] = jnp.zeros_like(dt_pad)
    dt_pad[0:ROWS, 0:HEADS] = step
    dt_pad[ROWS:, 0:HEADS] = step * -jnp.exp(a_log[...])
    size = dt_pad[0:ROWS]
    cum = dt_pad[ROWS:]
    row = rows_of((ROWS, 128))
    for shift in (1, 2, 4, 8, 16, 32):
        cum = cum + jnp.where(row >= shift, pltpu.roll(cum, shift, 0), 0.0)

    lane = lanes_of((ROWS, 128))
    left = lane < 64
    source = jnp.where(left, lane, lane - 64)
    causal = row >= source
    diagonal = row == source
    twice_b = jnp.concatenate([coeff_b, coeff_b], axis=0)
    scores = lax.dot_general(
        coeff_c, twice_b, (((1,), (1,)), ((), ())), preferred_element_type=F32
    )
    squares = jnp.zeros((ROWS, 128), F32)
    for pair in range(PAIRS):
        cols = slice(pair * 128, pair * 128 + 128)
        first, second = 2 * pair, 2 * pair + 1

        def spread(values):
            return jnp.where(left, values[:, first : first + 1], values[:, second : second + 1])

        acc = win_x[TOP - 3 : TOP - 3 + ROWS, cols] * wx[0:1, cols]
        for k in range(1, TAPS):
            acc += win_x[TOP - 3 + k : TOP - 3 + k + ROWS, cols] * wx[k : k + 1, cols]
        x_conv = acc / (1.0 + jnp.exp(-acc))
        cum_here = spread(cum)
        x_size = x_conv * spread(size)
        cum_source = jnp.sum(jnp.where(diagonal, cum_here, 0.0), axis=0, keepdims=True)
        decay = jnp.where(causal, jnp.exp(jnp.where(causal, cum_here - cum_source, 0.0)), 0.0)
        weights = (decay * scores).astype(BF16)
        blocks = jnp.concatenate(
            [jnp.where(left, x_size, 0.0), jnp.where(left, 0.0, x_size)], axis=0
        ).astype(BF16)
        y = jnp.dot(weights, blocks, preferred_element_type=F32)
        held = load_state(pair)
        y += jnp.exp(cum_here) * lax.dot_general(
            coeff_c, held, (((1,), (1,)), ((), ())), preferred_element_type=F32
        )
        y += spread(d_skip[...]) * x_conv
        if store_state is not None:
            last = cum_here[ROWS - 1 : ROWS, :]
            tail = (jnp.exp(last - cum_here) * x_size).astype(BF16)
            update = lax.dot_general(
                tail, coeff_b, (((0,), (0,)), ((), ())), preferred_element_type=F32
            )
            final = jnp.exp(cum[ROWS - 1 : ROWS, :])
            keep = jnp.where(
                rows_of((128, 128)) < 64, final[:, first : first + 1], final[:, second : second + 1]
            )
            store_state(pair, held.astype(F32) * keep + update)
        gate = z_ref[0, :, cols].astype(F32)
        g = y * (gate / (1.0 + jnp.exp(-gate)))
        gated[:, cols] = g
        squares += g * g
    scale = lax.rsqrt(jnp.sum(squares, axis=1, keepdims=True) * (1.0 / INNER) + 1e-05)
    normed[pl.ds(slot * ROWS, ROWS), :] = (gated[...] * scale * norm_w[...]).astype(BF16)


def load_pairs(win_bc, bc):
    both = bc[0].astype(F32)
    win_bc[TOP:, :STATE] = both[:, 0, :]
    win_bc[TOP:, STATE:] = both[:, 1, :]


def project(blocks, normed, weight, sent, kept):
    width = sent.shape[2]
    for at, out in ((0, sent), (NY, kept)):
        for k in range(NY):
            start = pl.multiple_of(blocks[at + k] * width, width)
            out[k] = jnp.dot(
                normed[...], weight[:, pl.ds(start, width)], preferred_element_type=F32
            ).astype(BF16)


def resident_kernel(
    count, blocks, out_w, state, conv_x, conv_bc, x, bc, z, dt,
    wx, wbc, dt_bias, a_log, d_skip, norm_w, parts, conv_rows, normed, weight,
    weight_sem, win_x, win_bc, dt_pad, gated,
):
    slot = pl.program_id(0)
    fetch = pltpu.make_async_copy(out_w, weight, weight_sem)

    @pl.when(slot == 0)
    def _():
        fetch.start()
        conv_rows[...] = conv_x[...].astype(F32)

    @pl.when(slot < count[0])
    def _():
        for k in range(TAPS - 1):
            win_x[TOP - 3 + k : TOP - 2 + k, :] = conv_rows[k, pl.ds(slot, 1), :]
        win_x[TOP:, :] = x[0].astype(F32)
        for k in range(TAPS - 1):
            both = conv_bc[0, k].astype(F32)
            for part in range(2):
                win_bc[TOP - 3 + k : TOP - 2 + k, part * STATE : part * STATE + STATE] = both[
                    part : part + 1
                ]
        load_pairs(win_bc, bc)

        def load_state(pair):
            return state[0, 2 * pair : 2 * pair + 2].reshape(128, STATE)

        mix_rows(
            win_x, win_bc, dt_pad, gated, dt, z,
            (wx, wbc, dt_bias, a_log, d_skip, norm_w), load_state, None, normed, slot,
        )

    @pl.when(slot >= count[0])
    def _():
        normed[pl.ds(slot * ROWS, ROWS), :] = jnp.zeros((ROWS, INNER), BF16)

    @pl.when(slot == pl.num_programs(0) - 1)
    def _():
        fetch.wait()
        project(blocks, normed, weight, parts.at[0:NY], parts.at[NY:])


ROW_SCRATCH = [
    pltpu.VMEM((TOP + ROWS, INNER), F32),
    pltpu.VMEM((TOP + ROWS, 2 * STATE), F32),
    pltpu.VMEM((2 * ROWS, 128), F32),
    pltpu.VMEM((ROWS, INNER), F32),
]


def whole(array):
    return pl.BlockSpec(array.shape, lambda *_: (0,) * array.ndim)


def per_slot(shape):
    return pl.BlockSpec((1,) + shape, lambda i, *_: (i,) + (0,) * len(shape))


def row_scratch(slots):
    return [
        pltpu.VMEM((slots * ROWS, INNER), BF16),
        pltpu.VMEM((INNER, 4096), BF16),
        pltpu.SemaphoreType.DMA,
    ] + ROW_SCRATCH


def partial_sums(slots):
    shape = (NY, slots * ROWS, 4096 // 8)
    return [jax.ShapeDtypeStruct(shape, BF16)] * 2


def resident_rows(count, blocks, out_w, state, conv_x, conv_bc, x, bc, z, dt, params):
    slots = state.shape[0]
    parts = jax.ShapeDtypeStruct((2 * NY, slots * ROWS, out_w.shape[1] // 8), BF16)
    return pl.pallas_call(
        resident_kernel,
        grid=(slots,),
        in_specs=[pl.BlockSpec(memory_space=pltpu.SMEM)] * 2
        + [pl.BlockSpec(memory_space=pl.ANY), per_slot(state.shape[1:]), whole(conv_x)]
        + [per_slot(a.shape[1:]) for a in (conv_bc, x, bc, z, dt)]
        + [whole(a) for a in params],
        out_specs=whole(parts),
        out_shape=parts,
        scratch_shapes=[pltpu.VMEM((TAPS - 1, slots, INNER), F32)] + row_scratch(slots),
        compiler_params=pltpu.CompilerParams(vmem_limit_bytes=VMEM_LIMIT),
        cost_estimate=pl.CostEstimate(
            flops=3_000_000_000, bytes_accessed=16_000_000, transcendentals=0
        ),
        name="resident_rows",
    )(count, blocks, out_w, state, conv_x, conv_bc, x, bc, z, dt, *params)


def line_hits(assign, target, column):
    target_z = lax.rem(target, NZ)
    return [
        (assign[column * NZ + lax.rem(target_z + NZ - offset, NZ)] == target).astype(jnp.int32)
        for offset in ORDER
    ]


def send_ranks(hits, shift):
    seen = jnp.int32(0)
    if shift != 2:
        seen = 1 - functools.reduce(jnp.maximum, hits[: len(EARLY)])
    ranks = []
    for hit in hits:
        ranks.append(seen)
        seen = seen + hit
    return ranks


def forward_kernel(sends, offsets, info, *refs):
    packets = dict(zip(offsets, refs))
    outs, sems = refs[len(offsets) : -1], refs[-1]
    me = info[32]
    column, z = lax.div(me, NZ), lax.rem(me, NZ)
    todo = []
    for slot, (shift, wanted) in enumerate(sends):
        target = lax.rem(column + shift, NX) * NZ + z
        hits = line_hits(info, target, column)
        for offset, hit, rank in zip(ORDER, hits, send_ranks(hits, shift)):
            if offset in packets:
                todo.append(
                    ((hit == 1) & (rank == wanted),
                     pltpu.make_async_copy(packets[offset], outs[slot], sems.at[slot]))
                )
    if 4 not in offsets:
        slot = len(sends)
        even = lax.rem(z, 2) == 0
        for when, offset in ((even, 2), (jnp.logical_not(even), 6)):
            todo.append(
                (when, pltpu.make_async_copy(packets[offset], outs[slot], sems.at[slot]))
            )
    for wanted, copy in todo:
        pl.when(wanted)(copy.start)
    for wanted, copy in todo:
        pl.when(wanted)(copy.wait)


def forward(sends, offsets, info, packets):
    count = len(sends) + (0 if 4 in offsets else 1)
    return pl.pallas_call(
        functools.partial(forward_kernel, sends, offsets),
        in_specs=[pl.BlockSpec(memory_space=pltpu.SMEM)]
        + [pl.BlockSpec(memory_space=pl.ANY)] * len(packets),
        out_specs=[pl.BlockSpec(memory_space=pltpu.VMEM)] * count,
        out_shape=[jax.ShapeDtypeStruct((PACK, 128), BF16)] * count,
        scratch_shapes=[pltpu.SemaphoreType.DMA((count,))],
        cost_estimate=pl.CostEstimate(flops=0, bytes_accessed=3_000_000, transcendentals=0),
        name="forward",
    )(info, *packets)


def blank_kernel(info, *outs):
    pass


def blank(info, count):
    return pl.pallas_call(
        blank_kernel,
        in_specs=[pl.BlockSpec(memory_space=pltpu.SMEM)],
        out_specs=[pl.BlockSpec(memory_space=pl.ANY)] * count,
        out_shape=[jax.ShapeDtypeStruct((PACK, 128), BF16)] * count,
        name="blank",
    )(info)


PACKETS = len(ORDER)
ARRIVED = len(SENDS)


def slot_kernel(info, blocks, out_w, *refs):
    line, rest = refs[:PACKETS], refs[PACKETS:]
    came, rest = rest[:ARRIVED], rest[ARRIVED:]
    (x, bc, z, dt, wx, wbc, dt_bias, a_log, d_skip, norm_w, sent, kept, state,
     held, valid, sems, normed, weight, weight_sem, win_x, win_bc, dt_pad, gated) = rest
    fetch = pltpu.make_async_copy(out_w, weight, weight_sem)
    packets = dict(zip(ORDER, line))
    arrived = dict(zip(SENDS, came))
    slot = pl.program_id(0)
    me = info[32]
    column, my_z = lax.div(me, NZ), lax.rem(me, NZ)

    @pl.when(slot == 0)
    def _():
        before = jnp.int32(0)
        for request in range(NX * NZ):
            valid[request] = before
            before = before + (info[request] == me).astype(jnp.int32)
        valid[NX * NZ] = before
        for shift in range(NX):
            sender = lax.rem(column + NX - shift, NX)
            hits = line_hits(info, me, sender)
            for offset, hit, rank in zip(ORDER, hits, send_ranks(hits, shift)):
                source = sender * NZ + lax.rem(my_z + NZ - offset, NZ)
                place = valid[source]

                @pl.when(hit == 1)
                def _(shift=shift, offset=offset, rank=rank, place=place):
                    if shift == 0:
                        pltpu.make_async_copy(
                            packets[offset], held.at[place], sems.at[place]
                        ).start()
                    for (over, n), packet in arrived.items():
                        if over == shift:
                            @pl.when(rank == n)
                            def _(packet=packet):
                                pltpu.make_async_copy(
                                    packet, held.at[place], sems.at[place]
                                ).start()
        fetch.start()

    live = slot < valid[NX * NZ]

    @pl.when(live)
    def _():
        win_x[TOP:, :] = x[0].astype(F32)
        load_pairs(win_bc, bc)
        pltpu.make_async_copy(held.at[slot], held.at[slot], sems.at[slot]).wait()
        conv = held[slot, 1024:PACK, :].astype(F32)
        for k in range(TAPS - 1):
            for b in range(8):
                win_x[TOP - 3 + k : TOP - 2 + k, 128 * b : 128 * b + 128] = conv[
                    8 * k + b : 8 * k + b + 1
                ]
            for b in range(2):
                win_bc[TOP - 3 + k : TOP - 2 + k, 128 * b : 128 * b + 128] = conv[
                    24 + 2 * k + b : 25 + 2 * k + b
                ]

        def load_state(pair):
            return held[slot, 128 * pair : 128 * pair + 128, :]

        def store_state(pair, value):
            state[0, 2 * pair : 2 * pair + 2] = value.astype(BF16).reshape(2, 64, STATE)

        mix_rows(
            win_x, win_bc, dt_pad, gated, dt, z,
            (wx, wbc, dt_bias, a_log, d_skip, norm_w), load_state, store_state, normed, slot,
        )

    @pl.when(jnp.logical_not(live))
    def _():
        normed[pl.ds(slot * ROWS, ROWS), :] = jnp.zeros((ROWS, INNER), BF16)
        state[...] = jnp.zeros_like(state)

    @pl.when(slot == pl.num_programs(0) - 1)
    def _():
        fetch.wait()
        project(blocks, normed, weight, sent, kept)


def slot_rows(info, blocks, out_w, line, came, x, bc, z, dt, params):
    slots = x.shape[0]
    sums = partial_sums(slots)
    return pl.pallas_call(
        slot_kernel,
        grid=(slots,),
        in_specs=[pl.BlockSpec(memory_space=pltpu.SMEM)] * 2
        + [pl.BlockSpec(memory_space=pl.ANY)] * (1 + PACKETS + ARRIVED)
        + [per_slot(a.shape[1:]) for a in (x, bc, z, dt)]
        + [whole(a) for a in params],
        out_specs=[whole(a) for a in sums] + [per_slot((HEADS, 64, STATE))],
        out_shape=sums + [jax.ShapeDtypeStruct((slots, HEADS, 64, STATE), BF16)],
        scratch_shapes=[
            pltpu.VMEM((CAP, PACK, 128), BF16),
            pltpu.SMEM((NX * NZ + 1,), jnp.int32),
            pltpu.SemaphoreType.DMA((CAP,)),
        ]
        + row_scratch(slots),
        compiler_params=pltpu.CompilerParams(vmem_limit_bytes=VMEM_LIMIT),
        cost_estimate=pl.CostEstimate(
            flops=3_000_000_000, bytes_accessed=20_000_000, transcendentals=0
        ),
        name="slot_rows",
    )(info, blocks, out_w, *line, *came, x, bc, z, dt, *params)


def across_cores(array):
    return lax.ppermute(array, "tp", [(t, t ^ 1) for t in range(2 * NY)])


def chip_sums(own, from_mate):
    return [own[k].astype(F32) + from_mate[k].astype(F32) for k in range(NY)]


def reduce_out(chip, slots):
    total = chip[0]
    for k in range(1, NY):
        shifted = [(t, (t + 2 * k) % (2 * NY)) for t in range(2 * NY)]
        total = total + lax.ppermute(chip[k].astype(BF16), "tp", shifted).astype(F32)
    return total.astype(BF16).reshape(slots, ROWS, -1)


def along_z(array, step):
    pairs = [(x * NZ + z, x * NZ + (z + step) % NZ) for x in range(NX) for z in range(NZ)]
    return lax.ppermute(array, "rep", pairs)


def across_z(array):
    pairs = [
        (x * NZ + z, x * NZ + (z + (2 if z % 2 == 0 else -2)) % NZ)
        for x in range(NX) for z in range(NZ)
    ]
    return lax.ppermute(array, "rep", pairs)


def along_x(sends, arrays):
    return [
        lax.ppermute(
            array, "rep",
            [(x * NZ + z, (x + shift) % NX * NZ + z) for x in range(NX) for z in range(NZ)],
        )
        for (shift, _), array in zip(sends, arrays)
    ]


def on_device(
    res_state, res_conv_x, res_conv_bc, res_x, res_bc, res_z, res_dt, res_count,
    hand_state, hand_conv_x, hand_conv_bc, slot_x, slot_bc, slot_z, slot_dt,
    assignment, conv_wx, conv_wbc, dt_bias, a_log, d_skip, norm_w, out_w,
):
    me = lax.axis_index("rep")
    tp = lax.axis_index("tp")
    info = jnp.concatenate([assignment, me[None].astype(jnp.int32)])
    packet = jnp.concatenate(
        [
            hand_state.reshape(-1, STATE),
            hand_conv_x.reshape(-1, STATE),
            hand_conv_bc.reshape(-1, STATE),
            jnp.zeros((2, STATE), BF16),
        ],
        axis=0,
    )
    up1, down1 = along_z(packet, 1), along_z(packet, -1)
    up2, down2 = along_z(packet, 2), along_z(packet, -2)

    params = (
        conv_wx, conv_wbc, dt_bias[None], a_log[None], d_skip[None],
        norm_w[None],
    )
    chip, core = tp // 2, tp % 2
    turns = (chip + jnp.arange(NY, dtype=jnp.int32)) % NY
    blocks = jnp.concatenate([2 * turns + 1 - core, 2 * turns + core])
    res_blocks = jnp.arange(2 * NY, dtype=jnp.int32)
    res_parts = resident_rows(
        res_count, res_blocks, out_w, res_state, res_conv_x.transpose(1, 0, 2),
        res_conv_bc, res_x, res_bc, res_z, res_dt.transpose(0, 2, 1), params,
    )
    up1, down1, up2, down2, res_parts = lax.optimization_barrier(
        (up1, down1, up2, down2, res_parts)
    )
    early = [packet, up1, down1, up2, down2]
    *ahead, far = forward(FIRST, EARLY, info, early)
    far = across_z(far)
    up3, down3 = along_z(up2, 1), along_z(down2, -1)
    first = along_x(FIRST, ahead)
    up3, down3, far, *first = lax.optimization_barrier((up3, down3, far, *first))
    line = early + [up3, down3, far]
    ahead = forward(SECOND, ORDER, info, line)
    *ahead, info, res_parts = lax.optimization_barrier((*ahead, info, res_parts))
    res_parts = lax.all_to_all(res_parts, "tp", 0, 0, tiled=True)
    second = along_x(SECOND, ahead)

    ids = jnp.arange(NX * NZ)
    goes = assignment[None, :] == ids[:, None]
    offset = (ids[:, None] - ids[None, :]) % NZ
    far = (offset > 2) & (offset < 6)
    all_hits = jnp.sum(goes.reshape(-1, NX, NZ), axis=2)
    near_hits = jnp.sum((goes & ~far).reshape(-1, NX, NZ), axis=2)
    shift = (ids[:, None] // NZ - jnp.arange(NX)[None, :]) % NX
    room = jnp.where(shift == 2, 2, jnp.where(shift == 0, NZ, 1 + jnp.minimum(near_hits, 1)))
    more = jnp.any(all_hits > room)
    third = lax.cond(
        more,
        lambda *held: tuple(along_x(SPARE, forward(SPARE, ORDER, held[0], held[1:]))),
        lambda *held: tuple(blank(held[0], len(SPARE))),
        info, *line,
    )
    res_out = jnp.sum(res_parts.astype(F32), axis=0).astype(BF16)
    res_out = res_out.reshape(res_state.shape[0], ROWS, -1)
    sent, kept, slot_state = slot_rows(
        info, blocks, out_w, line, first + second + list(third), slot_x, slot_bc, slot_z,
        slot_dt.transpose(0, 2, 1), params,
    )
    slot_out = reduce_out(chip_sums(kept, across_cores(sent)), slot_x.shape[0])
    return res_out, slot_out, slot_state


def solution(mesh):
    rows = P("rep", None, "tp")
    pairs = P("rep", None, None, "tp")
    states = P("rep", "tp", None, None)
    return jax.shard_map(
        on_device,
        mesh=mesh,
        in_specs=(
            states, rows, pairs, rows, pairs, rows, rows, P("rep"),
            states, rows, pairs, rows, pairs, rows, rows,
            P(), P(None, "tp"), P(None, None, "tp"), P("tp"), P("tp"), P("tp"), P("tp"),
            P("tp", None),
        ),
        out_specs=(rows, rows, states),
        check_vma=False,
    )
```
